256 devices in a mesh: clip: 2 (over core), seq: 128 (over x, z, y).
Axes of the slice: x: 4, y: 4, z: 8, core: 2. Of those that a mesh axis runs over, the one named last changes fastest.
Arguments:
- latents: bfloat16 [256, 128, 1280], P(('clip', 'seq')), parts along dimension 0, may hold values from -6 to 6
- ref_hidden: bfloat16 [256, 1280], P(('clip', 'seq')), parts along dimension 0, may hold values from -6 to 6
- gain_spatial: float32 [1280], replicated, may hold values from 0.25 to 1.75
- w_qkv_spatial: bfloat16 [1280, 1920], P(None, 'seq'), may hold values from -8 to 8
- w_out_spatial: bfloat16 [640, 1280], P(None, 'seq'), may hold values from -0.25 to 0.25
- temporal_norm_gain: float32 [1280], replicated, may hold values from 0.25 to 1.75
- w_qkv_temporal: bfloat16 [1280, 1920], P(None, 'seq'), may hold values from -8 to 8
- w_out_temporal: bfloat16 [640, 1280], P(None, 'seq'), may hold values from -0.25 to 0.25
Outputs:
- mixed: bfloat16 [256, 128, 1280], P(('clip', 'seq')), parts along dimension 0
The draws below stay inside these ranges and needn't reach their ends.
There are 2 independent parts, one for each index of `clip`. The reference program is written for one: setup_inputs(seed, part) draws one part's arguments, and reference() takes and returns one part's arrays. A program takes and returns all parts, laid end to end along the dimension named above; an argument that names none is the same for every part. Nothing has to cross between parts.
All inputs are finite; a program needn't handle non-finite values.
Results may differ from the reference program's by a relative error of at most 0.0095.
Values may be sent and summed in bfloat16 or wider, within the bound.
No kernel may reach another device: no remote copies, remote signals or barrier semaphores. Data moves between devices by JAX's collectives and lax.ppermute only.
A program may use at most 64 MiB of HBM per device.

```python
import jax
import jax.numpy as jnp
from jax import lax

D = 1280
HEADS = 10
HEAD = 64
PIX = 128
INNER = 640
FRAMES = 128


def qkv_matrix(key):
    key_base, key_query, key_value = jax.random.split(key, 3)
    softmax_scale_factor = D ** (-0.5)
    base_keys = jax.random.truncated_normal(key_base, -4.0, 4.0, (D, INNER), jnp.float32) * softmax_scale_factor
    fresh = jax.random.truncated_normal(key_query, -4.0, 4.0, (D, INNER), jnp.float32) * softmax_scale_factor
    value_part = jax.random.truncated_normal(key_value, -4.0, 4.0, (D, INNER), jnp.float32) * softmax_scale_factor
    query_part = fresh
    return jnp.concatenate([query_part, base_keys, value_part], axis=1).astype(jnp.bfloat16)


def draw_w_qkv_spatial(key, part):
    key = jax.random.fold_in(key, 1)
    return qkv_matrix(key)


def draw_w_qkv_temporal(key, part):
    key = jax.random.fold_in(key, 2)
    return qkv_matrix(key)


def levels(stream_key, dims, shards, least, top_value):
    def one(axis_at, parts):
        heights = jax.random.uniform(jax.random.fold_in(jax.random.fold_in(stream_key, 6), axis_at), (parts,), jnp.float32, least / len(shards), top_value / len(shards))
        return jnp.repeat(jnp.exp(heights), dims[axis_at] // parts).reshape((-1,) + (1,) * (len(dims) - axis_at - 1))

    factor_of = one(*shards[0])
    for cut in shards[1:]:
        factor_of = factor_of * one(*cut)
    return factor_of


def bell_draw(rng, shape, width, limit, pieces=(), dtype=jnp.bfloat16):
    loudness = levels(rng, shape, pieces, -0.22, 0.18) if pieces else 1.0
    result = jax.random.normal(rng, shape, jnp.float32) * width * loudness
    return jnp.minimum(jnp.maximum(result, -limit), limit).astype(dtype)


def setup_inputs(seed: int = 0, part: int = 0) -> dict:
    splits = jax.random.split(jax.random.key(seed), 9)
    own_keys = jax.random.split(jax.random.fold_in(splits[8], part), 9)
    latents = bell_draw(own_keys[0], (FRAMES, PIX, D), 1.0, 6.0, ((0, 128),))
    ref_hidden = bell_draw(own_keys[1], (PIX, D), 1.0, 6.0, ((0, 128),))
    gain_spatial = jnp.clip(1.0 + 0.15 * jax.random.normal(splits[2], (D,), jnp.float32), 0.25, 1.75)
    w_qkv_spatial = draw_w_qkv_spatial(jax.random.fold_in(splits[8], 71), part)
    w_out_spatial = bell_draw(splits[4], (INNER, D), INNER ** -0.5, 0.25, ((1, 128),))
    temporal_norm_gain = jnp.clip(1.0 + 0.15 * jax.random.normal(splits[5], (D,), jnp.float32), 0.25, 1.75)
    w_qkv_temporal = draw_w_qkv_temporal(jax.random.fold_in(splits[8], 71), part)
    w_out_temporal = bell_draw(splits[7], (INNER, D), INNER ** -0.5, 0.25, ((1, 128),))
    return {"latents": latents, "ref_hidden": ref_hidden, "gain_spatial": gain_spatial, "w_qkv_spatial": w_qkv_spatial, "w_out_spatial": w_out_spatial, "temporal_norm_gain": temporal_norm_gain, "w_qkv_temporal": w_qkv_temporal, "w_out_temporal": w_out_temporal}


epsilon = 1e-05

def layer_norm(states, scale_gain):
    widened = states.astype(jnp.float32)
    average = lax.optimization_barrier(jnp.mean(widened, axis=-1, keepdims=True))
    spread = lax.optimization_barrier(jnp.mean((widened - average) ** 2, axis=-1, keepdims=True))
    return ((widened - average) * lax.rsqrt(spread + epsilon) * scale_gain).astype(jnp.bfloat16)

def attend(queries, keys_all, values):
    softmax_scale_factor = HEAD ** (-0.5)

    def one_head(operands):
        per_head_queries, per_head_keys, per_head_values = operands
        attention_logits = jnp.einsum('haf,hgf->hag', per_head_queries.astype(jnp.float32), per_head_keys.astype(jnp.float32)) * softmax_scale_factor
        top = lax.optimization_barrier(jnp.max(attention_logits, axis=-1, keepdims=True))
        expo = jnp.exp(attention_logits - top)
        attention_probabilities = (expo / lax.optimization_barrier(jnp.sum(expo, axis=-1, keepdims=True))).astype(jnp.bfloat16)
        return jnp.einsum('pzt,ptg->pzg', attention_probabilities.astype(jnp.float32), per_head_values.astype(jnp.float32)).astype(jnp.bfloat16)
    heads_first = lax.map(one_head, (queries.transpose(2, 0, 1, 3), keys_all.transpose(2, 0, 1, 3), values.transpose(2, 0, 1, 3)))
    return heads_first.transpose(1, 2, 0, 3)

def reference(latents, ref_hidden, gain_spatial, w_qkv_spatial, w_out_spatial, temporal_norm_gain, w_qkv_temporal, w_out_temporal):
    normed = layer_norm(latents, gain_spatial).reshape(FRAMES * PIX, D)
    frame_qkv = jnp.dot(normed, w_qkv_spatial, preferred_element_type=jnp.float32).astype(jnp.bfloat16)
    frame_qkv = frame_qkv.reshape(FRAMES, PIX, 3, HEADS, HEAD)
    ref_kv = jnp.dot(ref_hidden, w_qkv_spatial[:, INNER:], preferred_element_type=jnp.float32).astype(jnp.bfloat16)
    ref_kv = ref_kv.reshape(PIX, 2, HEADS, HEAD)
    ref_keys = jnp.broadcast_to(ref_kv[None, :, 0], (FRAMES, PIX, HEADS, HEAD))
    ref_values = jnp.broadcast_to(ref_kv[None, :, 1], (FRAMES, PIX, HEADS, HEAD))
    keys_all = jnp.concatenate([frame_qkv[:, :, 1], ref_keys], axis=1)
    values_all = jnp.concatenate([frame_qkv[:, :, 2], ref_values], axis=1)
    spatial_attn = attend(frame_qkv[:, :, 0], keys_all, values_all).reshape(FRAMES * PIX, INNER)
    hidden = latents.reshape(FRAMES * PIX, D).astype(jnp.float32) + jnp.dot(spatial_attn, w_out_spatial, preferred_element_type=jnp.float32)
    hidden = hidden.astype(jnp.bfloat16)
    tnormed = layer_norm(hidden, temporal_norm_gain)
    temporal_qkv = jnp.dot(tnormed, w_qkv_temporal, preferred_element_type=jnp.float32).astype(jnp.bfloat16)
    temporal_qkv = temporal_qkv.reshape(FRAMES, PIX, 3, HEADS, HEAD).transpose(1, 0, 2, 3, 4)
    temporal_attn = attend(temporal_qkv[:, :, 0], temporal_qkv[:, :, 1], temporal_qkv[:, :, 2])
    temporal_attn = temporal_attn.transpose(1, 0, 2, 3).reshape(FRAMES * PIX, INNER)
    mixed = hidden.astype(jnp.float32) + jnp.dot(temporal_attn, w_out_temporal, preferred_element_type=jnp.float32)
    return mixed.astype(jnp.bfloat16).reshape(FRAMES, PIX, D)
```

```python
import functools
import itertools

import jax
import jax.numpy as jnp
from jax import lax
from jax.experimental import pallas as pl
from jax.experimental.pallas import tpu as pltpu
from jax.sharding import PartitionSpec as P

D = 1280
HEADS = 10
HEAD = 64
INNER = 640
PIX = 128
NX, NZ, NY = 4, 8, 4
SEQ = NX * NZ * NY
EPS = 1e-05
BF = jnp.bfloat16
F32 = jnp.float32
SHIFTS = (0, 1, 3, 2)
T_S, T_O, T_T, T_U = 6, 3, 5, 3
TILES = T_S + T_O + T_T + T_U


def seq_of(x, z, y):
    return (x * NZ + z) * NY + y


Z_GROUPS = [[seq_of(x, z, y) for z in range(NZ)] for x in range(NX) for y in range(NY)]
SWAP = [(i, (i + SEQ) % (2 * SEQ)) for i in range(2 * SEQ)]


def ring_perm(k, stage):
    pairs = []
    for c, x, z, y in itertools.product(range(2), range(NX), range(NZ), range(NY)):
        if (c + stage) % 2 == 0:
            to = ((x + k) % NX, z, y)
        else:
            to = (x, z, (y + k) % NY)
        pairs.append((c * SEQ + seq_of(x, z, y), c * SEQ + seq_of(*to)))
    return pairs


def ring(block, stage):
    return [block] + [
        lax.ppermute(block, ("clip", "seq"), ring_perm(k, stage)) for k in SHIFTS[1:]
    ]


def swap(block):
    return lax.ppermute(block, ("clip", "seq"), SWAP)


def vmem(n):
    return [pl.BlockSpec(memory_space=pltpu.VMEM)] * n


PARAMS = pltpu.CompilerParams(vmem_limit_bytes=48 * 1024 * 1024)


def layer_norm(x, gain):
    mean = jnp.mean(x, axis=-1, keepdims=True)
    d = x - mean
    var = jnp.mean(d * d, axis=-1, keepdims=True)
    return (d * lax.rsqrt(var + EPS) * gain).astype(BF)


def pack_kernel(ws, ref, wo, wt, wu, out):
    c = lax.axis_index("clip")

    def tile(*rows):
        n = sum(r.shape[0] for r in rows)
        parts = [r.astype(F32) for r in rows]
        if n < 16:
            parts.append(jnp.zeros((16 - n, 128), F32))
        return jnp.concatenate(parts, axis=0).astype(BF)

    def fill(half):
        at = 0
        for t in range(5):
            out[at] = tile(ws[:, 640 * half + 128 * t : 640 * half + 128 * (t + 1)])
            at += 1
        out[at] = tile(*[ref[:, 128 * u : 128 * (u + 1)] for u in range(10)])
        at += 1
        for t in range(3):
            out[at] = tile(wo[:, 256 * half + 128 * t : 256 * half + 128 * (t + 1)])
            at += 1
        for t in range(5):
            out[at] = tile(wt[:, 640 * half + 128 * t : 640 * half + 128 * (t + 1)])
            at += 1
        for t in range(3):
            out[at] = tile(wu[:, 256 * half + 128 * t : 256 * half + 128 * (t + 1)])
            at += 1

    for half in range(2):
        pl.when(c == half)(functools.partial(fill, half))


def place():
    s = lax.axis_index("seq")
    return lax.axis_index("clip"), s // (NZ * NY), lax.rem(s, NY)


def lanes(ref, start, tiles, first):
    parts = [ref[start : start + 8, first + t].reshape(128, 128) for t in range(tiles)]
    return jnp.concatenate(parts, axis=1)


def project(own, oth, acc, xa, xb, tiles_a, tiles_b, first_b):
    c, x, y = place()
    for j in range(4):
        wa = jnp.concatenate([lanes(own[j], 8 * i, tiles_a, 0) for i in range(4)], axis=0)
        wb = jnp.concatenate([lanes(oth[i], 8 * j, tiles_b, first_b) for i in range(4)], axis=0)
        dims = (((1,), (1,)), ((), ()))
        r = lax.dot_general(wa, xa, dims, preferred_element_type=F32)
        r = r + lax.dot_general(wb, xb, dims, preferred_element_type=F32)
        for i in range(4):
            first, second = SHIFTS[i], SHIFTS[j]
            dx = jnp.where(c == 0, first, second)
            dy = jnp.where(c == 0, second, first)
            xs = lax.rem(x - dx + NX, NX)
            ys = lax.rem(y - dy + NY, NY)
            for z in range(NZ):
                at = (i * 8 + z) * 16
                acc[xs, z, ys] = r[at : at + 16]


def compact(acc, rows, count):
    for s in range(SEQ):
        x, z, y = s // 32, (s // 4) % 8, s % 4
        rows[count * s : count * (s + 1), :] = acc[x, z, y, 0:count, :]


def halves(xv, c):
    lo, hi = xv[:, :640], xv[:, 640:]
    first = c == 0
    return jnp.where(first, lo, hi), jnp.where(first, hi, lo)


def heads(rows, keys, attn):
    for h in range(HEADS):
        q = rows[64 * h : 64 * (h + 1), 0:128].astype(BF)
        k = rows[640 + 64 * h : 640 + 64 * (h + 1), 0:keys].astype(BF)
        v = rows[1280 + 64 * h : 1280 + 64 * (h + 1), 0:keys].astype(BF)
        st = lax.dot_general(k, q, (((0,), (0,)), ((), ())), preferred_element_type=F32)
        st = st * (HEAD**-0.5)
        e = jnp.exp(st - jnp.max(st, axis=0, keepdims=True))
        p = (e * (1.0 / jnp.sum(e, axis=0, keepdims=True))).astype(BF)
        attn[64 * h : 64 * (h + 1), :] = jnp.dot(v, p, preferred_element_type=F32)


def spatial_kernel(*refs):
    own, oth = refs[0:4], refs[4:8]
    latents, gain, out, acc, rows, wide, attn = refs[8:]
    c, _, _ = place()
    normed = layer_norm(latents[...].astype(F32), gain[...])
    for j in range(4):
        for i in range(4):
            wide[j * 512 + i * 128 : j * 512 + (i + 1) * 128, :] = (
                own[j][8 * i : 8 * i + 8, 5].reshape(128, 128).astype(F32)
            )
    ref_hidden = jnp.concatenate(
        [wide[pl.ds(u, 128, stride=16), :] for u in range(10)], axis=1
    ).astype(BF)
    xa, xb = halves(jnp.concatenate([normed, ref_hidden], axis=0), c)
    project(own, oth, acc, xa, xb, 5, 5, 0)
    compact(acc, rows, 15)
    heads(rows, 256, attn)
    out[...] = attn[...].T.astype(BF)


def temporal_kernel(*refs):
    own, oth = refs[0:4], refs[4:8]
    tokens, out, acc, rows, attn = refs[8:]
    c, _, _ = place()
    xa, xb = halves(tokens[...], c)
    project(own, oth, acc, xa, xb, 5, 5, 0)
    compact(acc, rows, 15)
    heads(rows, 128, attn)
    out[...] = attn[...].T.astype(BF)


def out_project(own, oth, attn, acc, rows, first):
    c, _, _ = place()
    a = attn[...]
    xa = jnp.where(c == 0, a[:, 0:384], a[:, 256:640])
    xb = jnp.where(c == 0, a[:, 384:640], a[:, 0:256])
    project(own, oth, acc, xa, xb, 3, 2, first + (1 - c))
    compact(acc, rows, 10)
    return rows[...].T


def hidden_kernel(*refs):
    own, oth = refs[0:4], refs[4:8]
    attn, latents, gain, hidden, tnormed, acc, rows = refs[8:]
    total = latents[...].astype(F32) + out_project(own, oth, attn, acc, rows, 0)
    h = total.astype(BF)
    hidden[...] = h
    tnormed[...] = layer_norm(h.astype(F32), gain[...])


def mixed_kernel(*refs):
    own, oth = refs[0:4], refs[4:8]
    attn, hidden, mixed, acc, rows = refs[8:]
    total = hidden[...].astype(F32) + out_project(own, oth, attn, acc, rows, 0)
    mixed[...] = total.astype(BF)


def call(kernel, args, outs, scratch, name, flops=0):
    shapes = [jax.ShapeDtypeStruct(s, BF) for s in outs]
    single = len(shapes) == 1
    size = sum(a.size * a.dtype.itemsize for a in args) + sum(2 * s.size for s in shapes)
    return pl.pallas_call(
        kernel,
        out_shape=shapes[0] if single else shapes,
        in_specs=vmem(len(args)),
        out_specs=vmem(1)[0] if single else vmem(len(shapes)),
        scratch_shapes=[pltpu.VMEM(s, F32) for s in scratch],
        compiler_params=PARAMS,
        cost_estimate=pl.CostEstimate(flops=flops, bytes_accessed=size, transcendentals=0),
        name=name,
    )(*args)


def body(latents, ref_hidden, gain_s, w_s, w_o, gain_t, w_t, w_u):
    latents = latents.reshape(PIX, D)
    gain_s = gain_s.reshape(1, D)
    gain_t = gain_t.reshape(1, D)
    packed = call(
        pack_kernel, [w_s.T, ref_hidden, w_o.T, w_t.T, w_u.T], [(TILES, 16, 128)], [], "pack"
    )
    along_z = lax.all_to_all(
        jnp.broadcast_to(packed[None], (NZ, TILES, 16, 128)),
        "seq",
        0,
        0,
        axis_index_groups=Z_GROUPS,
        tiled=True,
    )
    n_spatial = T_S + T_O
    first = ring(along_z[:, :n_spatial], 0)
    part_s = jnp.concatenate([b[:, :T_S] for b in first], axis=0)
    part_o = jnp.concatenate([b[:, T_S:] for b in first], axis=0)
    own_s = ring(part_s, 1)
    oth_s = [swap(b) for b in own_s]
    own_o = ring(part_o, 1)
    oth_o = [swap(b) for b in own_o]
    part_t = jnp.concatenate(ring(along_z[:, n_spatial:], 0), axis=0)
    own_t = ring(part_t, 1)
    oth_t = [swap(b) for b in own_t]

    attn = call(
        spatial_kernel,
        own_s + oth_s + [latents, gain_s],
        [(PIX, INNER)],
        [(NX, NZ, NY, 16, 256), (1920, 256), (2048, 128), (INNER, 128)],
        "spatial",
        2 * 2048 * 256 * D,
    )
    hidden, tnormed = call(
        hidden_kernel,
        own_o + oth_o + [attn, latents, gain_t],
        [(PIX, D), (PIX, D)],
        [(NX, NZ, NY, 16, 128), (D, 128)],
        "hidden",
        2 * 2048 * 128 * INNER,
    )
    tokens = lax.all_to_all(tnormed, "seq", 0, 0, tiled=True)
    tattn = call(
        temporal_kernel,
        [b[:, :T_T] for b in own_t] + [b[:, :T_T] for b in oth_t] + [tokens],
        [(PIX, INNER)],
        [(NX, NZ, NY, 16, 128), (1920, 128), (INNER, 128)],
        "temporal",
        2 * 2048 * 128 * D,
    )
    back = lax.all_to_all(tattn, "seq", 0, 0, tiled=True)
    mixed = call(
        mixed_kernel,
        [b[:, T_T:] for b in own_t] + [b[:, T_T:] for b in oth_t] + [back, hidden],
        [(PIX, D)],
        [(NX, NZ, NY, 16, 128), (D, 128)],
        "mixed",
        2 * 2048 * 128 * INNER,
    )
    return mixed.reshape(1, PIX, D)


def solution(mesh):
    in_specs = (
        P(("clip", "seq"), None, None),
        P(("clip", "seq"), None),
        P(),
        P(None, "seq"),
        P(None, "seq"),
        P(),
        P(None, "seq"),
        P(None, "seq"),
    )
    out_specs = P(("clip", "seq"), None, None)
    return jax.shard_map(body, mesh=mesh, in_specs=in_specs, out_specs=out_specs, check_vma=False)
```

```python
import functools
import itertools

import jax
import jax.numpy as jnp
from jax import lax
from jax.experimental import pallas as pl
from jax.experimental.pallas import tpu as pltpu
from jax.sharding import PartitionSpec as P

D = 1280
HEADS = 10
HEAD = 64
INNER = 640
PIX = 128
NX, NZ, NY = 4, 8, 4
SEQ = NX * NZ * NY
EPS = 1e-05
BF = jnp.bfloat16
F32 = jnp.float32
SHIFTS = (0, 1, 3, 2)
GROUP = 7
TILES = 2 * GROUP


def seq_of(x, z, y):
    return (x * NZ + z) * NY + y


Z_GROUPS = [[seq_of(x, z, y) for z in range(NZ)] for x in range(NX) for y in range(NY)]
SWAP = [(i, (i + SEQ) % (2 * SEQ)) for i in range(2 * SEQ)]


def ring_perm(k, stage):
    pairs = []
    for c, x, z, y in itertools.product(range(2), range(NX), range(NZ), range(NY)):
        if (c + stage) % 2 == 0:
            to = ((x + k) % NX, z, y)
        else:
            to = (x, z, (y + k) % NY)
        pairs.append((c * SEQ + seq_of(x, z, y), c * SEQ + seq_of(*to)))
    return pairs


def ring(block, stage):
    return [block] + [
        lax.ppermute(block, ("clip", "seq"), ring_perm(k, stage)) for k in SHIFTS[1:]
    ]


def ring_by_halves(pair, stage):
    def shift(part, k):
        return lax.ppermute(part, ("clip", "seq"), ring_perm(k, stage))

    one, two = pair
    up_one, down_two = shift(one, 1), shift(two, 3)
    up_two, down_one = shift(two, 1), shift(one, 3)
    far_one, far_two = shift(up_one, 1), shift(down_two, 3)
    return [one, two, up_one, up_two, down_one, down_two, far_one, far_two]


def swap(block):
    return lax.ppermute(block, ("clip", "seq"), SWAP)


def vmem(n):
    return [pl.BlockSpec(memory_space=pltpu.VMEM)] * n


ANY = pl.BlockSpec(memory_space=pl.ANY)


def small(mib):
    return pltpu.CompilerParams(vmem_limit_bytes=mib * 1024 * 1024)


def layer_norm(x, gain):
    mean = jnp.mean(x, axis=-1, keepdims=True)
    d = x - mean
    var = jnp.mean(d * d, axis=-1, keepdims=True)
    return (d * lax.rsqrt(var + EPS) * gain).astype(BF)


def pack_kernel(ws_in, ref_in, wo_in, wt_in, wu_in, out, ws, ref, wo, wt, wu, sems):
    c = lax.axis_index("clip")
    pairs = ((ws_in, ws), (ref_in, ref), (wo_in, wo), (wt_in, wt), (wu_in, wu))
    copies = [pltpu.make_async_copy(src, dst, sems.at[i]) for i, (src, dst) in enumerate(pairs)]
    for copy in copies:
        copy.start()
    for copy in copies:
        copy.wait()

    def tile(*rows):
        n = sum(r.shape[0] for r in rows)
        parts = [r.astype(F32) for r in rows]
        if n < 16:
            parts.append(jnp.zeros((16 - n, 128), F32))
        return jnp.concatenate(parts, axis=0).astype(BF)

    def lane(ref, t):
        return ref[:, 128 * t : 128 * (t + 1)]

    def fill(half):
        refs = [lane(ref, u) for u in range(10)]
        for t in range(5):
            out[t] = tile(lane(ws, 5 * half + t), refs[t])
            out[GROUP + t] = tile(lane(wt, 5 * half + t))
        for at, w, extra in ((5, wo, refs[5:]), (GROUP + 5, wu, [])):
            middle = lane(w, 2).astype(F32)[5 * half : 5 * half + 5]
            out[at] = tile(lane(w, 3 * half), middle)
            out[at + 1] = tile(lane(w, 3 * half + 1), *extra)

    for half in range(2):
        pl.when(c == half)(functools.partial(fill, half))


def halves_kernel(along_z, p1, p2, p3, one, two):
    spatial = (along_z, p1, p2, p3)
    for half, out in enumerate((one, two)):
        for i in range(2):
            out[8 * i : 8 * i + 8] = spatial[2 * half + i][:, 0:GROUP]
        out[16:20] = along_z[4 * half : 4 * half + 4, GROUP : 2 * GROUP]


def temporal_blocks_kernel(*refs):
    out = refs[-1]
    for i, piece in enumerate(refs[:-1]):
        out[4 * i : 4 * i + 4] = piece[16:20]


def gate_kernel(*refs):
    pass


def gate(values, after):
    n = len(values)
    return list(
        pl.pallas_call(
            gate_kernel,
            out_shape=[jax.ShapeDtypeStruct(v.shape, v.dtype) for v in values],
            in_specs=vmem(n + 1),
            out_specs=vmem(n),
            input_output_aliases={i: i for i in range(n)},
            compiler_params=small(1),
            name="gate",
        )(*values, after)
    )


def reorder(kernel, args, outs, name):
    return pl.pallas_call(
        kernel,
        out_shape=[jax.ShapeDtypeStruct((n, GROUP, 16, 128), BF) for n in outs],
        in_specs=vmem(len(args)),
        out_specs=vmem(len(outs)),
        compiler_params=small(4),
        name=name,
    )(*args)


def to_rows(value, out, rows, n):
    wide = 2 * out.shape[1]
    for t in range(wide):
        at = pl.ds(t, 128, stride=wide)
        rows[at, :] = value[:, 128 * t : 128 * (t + 1)] if t < n else jnp.zeros((128, 128), F32)
    out.reshape(128 * wide, 128)[...] = rows[...].astype(BF)


def from_rows(ref, rows, n):
    wide = 2 * ref.shape[1]
    rows[...] = ref.reshape(128 * wide, 128)[...].astype(F32)
    return jnp.concatenate(
        [rows[pl.ds(t, 128, stride=wide), :] for t in range(n)], axis=1
    ).astype(BF)


def place():
    s = lax.axis_index("seq")
    return lax.axis_index("clip"), s // (NZ * NY), lax.rem(s, NY)


def blocks(refs, j, i):
    per_shift = len(refs) // 4
    at = 4 // per_shift
    return refs[per_shift * j + i // at], 8 * (i % at)


def lanes(refs, j, i, first, count):
    ref, start = blocks(refs, j, i)
    parts = [ref[start : start + 8, first + t].reshape(128, 128) for t in range(count)]
    return jnp.concatenate(parts, axis=1)


def pieces_of(own, oth, j, first, count):
    wa = [lanes(own, j, i, first, count) for i in range(4)]
    wb = [lanes(oth, i, j, first, count) for i in range(4)]
    return jnp.concatenate(wa, axis=0), jnp.concatenate(wb, axis=0)


def spread(acc, r, j, row, x_core):
    c, x, y = place()
    for i in range(4):
        dx = jnp.where(c == x_core, SHIFTS[i], SHIFTS[j])
        dy = jnp.where(c == x_core, SHIFTS[j], SHIFTS[i])
        xs = lax.rem(x - dx + NX, NX)
        ys = lax.rem(y - dy + NY, NY)
        for z in range(NZ):
            at = (i * 8 + z) * 16
            acc[xs, z, ys, row : row + 16, :] = r[at : at + 16]


NT = (((1,), (1,)), ((), ()))
NN = (((1,), (0,)), ((), ()))


def dot(a, b, dims):
    return lax.dot_general(a, b, dims, preferred_element_type=F32)


def qkv_project(own, oth, acc, rows, tokens, x_core):
    c, _, _ = place()
    xa, xb = halves(tokens, c)
    for j in range(4):
        wa, wb = pieces_of(own, oth, j, 0, 5)
        spread(acc, dot(wa, xa, NT) + dot(wb, xb, NT), j, 0, x_core)
    for s in range(SEQ):
        x, z, y = s // 32, (s // 4) % 8, s % 4
        rows[15 * s : 15 * s + 15, :] = acc[x, z, y, 0:15, :]


def out_project(own, oth, acc, rows, part, dims, x_core):
    c, _, _ = place()
    lo, mid, hi = part(0, 256), part(256, 384), part(384, 640)
    xa = jnp.where(c == 0, lo, hi)
    xb = jnp.where(c == 0, hi, lo)
    for j in range(4):
        wa, wb = pieces_of(own, oth, j, 5, 2)
        spread(acc, dot(wa, xa, dims) + dot(wb, xb, dims), j, 0, x_core)
        ma, mb = dot(wa[:, :128], mid, dims), dot(wb[:, :128], mid, dims)
        spread(acc, jnp.where(c == 0, ma, mb), j, 16, x_core)
        spread(acc, jnp.where(c == 0, mb, ma), j, 32, x_core)
    for s in range(SEQ):
        x, z, y = s // 32, (s // 4) % 8, s % 4
        m0 = acc[x, z, y, 26:31, :]
        m1 = acc[x, z, y, 42:47, :]
        rows[10 * s : 10 * s + 10, :] = acc[x, z, y, 0:10, :] + jnp.concatenate([m0, m1], axis=0)


def halves(xv, c):
    lo, hi = xv[:, :640], xv[:, 640:]
    first = c == 0
    return jnp.where(first, lo, hi), jnp.where(first, hi, lo)


def heads(rows, keys, attn):
    for h in range(HEADS):
        q = rows[64 * h : 64 * (h + 1), 0:128].astype(BF)
        k = rows[640 + 64 * h : 640 + 64 * (h + 1), 0:keys].astype(BF)
        v = rows[1280 + 64 * h : 1280 + 64 * (h + 1), 0:keys].astype(BF)
        st = lax.dot_general(k, q, (((0,), (0,)), ((), ())), preferred_element_type=F32)
        st = st * (HEAD**-0.5)
        e = jnp.exp(st - jnp.max(st, axis=0, keepdims=True))
        p = (e * (1.0 / jnp.sum(e, axis=0, keepdims=True))).astype(BF)
        attn[64 * h : 64 * (h + 1), :] = jnp.dot(v, p, preferred_element_type=F32)


def reference_tokens(own, last):
    parts = []
    for t in (0, 1, 2, 3, 4, 6):
        for j in range(4):
            for i in range(4):
                at = (j * 4 + i) * 64
                ref, start = blocks(own, j, i)
                tail = ref[start : start + 8, t].astype(F32)[:, 8:16, :]
                last[t, at : at + 64, :] = tail.reshape(64, 128)
        at = (7,) if t < 5 else (2, 3, 4, 5, 6)
        parts += [last[t, pl.ds(r, 128, stride=8), :] for r in at]
    return jnp.concatenate(parts, axis=1).astype(BF)


def spatial_kernel(*refs):
    own, oth = refs[0:8], refs[8:16]
    latents, gain_s, gain_t, hidden, tnormed, acc, rows, last, attn, acc_out, rows_out = refs[16:]
    normed = layer_norm(latents[...].astype(F32), gain_s[...])
    tokens = jnp.concatenate([normed, reference_tokens(own, last)], axis=0)
    qkv_project(own, oth, acc, rows, tokens, 0)
    heads(rows, 256, attn)
    part = lambda a, b: attn[a:b, :].astype(BF)
    out_project(own, oth, acc_out, rows_out, part, NN, 0)
    h = (latents[...].astype(F32) + rows_out[...].T).astype(BF)
    hidden[...] = h
    to_rows(layer_norm(h.astype(F32), gain_t[...]).astype(F32), tnormed, rows_out, 10)


def temporal_kernel(*refs):
    own, oth = refs[0:4], refs[4:8]
    tokens, out, acc, rows, attn, wide, wide_out = refs[8:]
    qkv_project(own, oth, acc, rows, from_rows(tokens, wide, 10), 1)
    heads(rows, 128, attn)
    to_rows(attn[...].T, out, wide_out, 5)


def mixed_kernel(*refs):
    own, oth = refs[0:4], refs[4:8]
    attn, hidden, mixed, acc, rows, wide = refs[8:]
    a = from_rows(attn, wide, 5)
    out_project(own, oth, acc, rows, lambda first, last: a[:, first:last], NT, 1)
    mixed[...] = (hidden[...].astype(F32) + rows[...].T).astype(BF)


def call(kernel, args, outs, scratch, name, flops, mib):
    shapes = [jax.ShapeDtypeStruct(s, BF) for s in outs]
    single = len(shapes) == 1
    size = sum(a.size * a.dtype.itemsize for a in args) + sum(2 * s.size for s in shapes)
    return pl.pallas_call(
        kernel,
        out_shape=shapes[0] if single else shapes,
        in_specs=vmem(len(args)),
        out_specs=vmem(1)[0] if single else vmem(len(shapes)),
        scratch_shapes=[pltpu.VMEM(s, F32) for s in scratch],
        compiler_params=small(mib),
        cost_estimate=pl.CostEstimate(flops=flops, bytes_accessed=size, transcendentals=0),
        name=name,
    )(*args)


def body(latents, ref_hidden, gain_s, w_s, w_o, gain_t, w_t, w_u):
    latents = latents.reshape(PIX, D)
    gain_s = gain_s.reshape(1, D)
    gain_t = gain_t.reshape(1, D)
    shards = [w_s.T, ref_hidden, w_o.T, w_t.T, w_u.T]
    packed = pl.pallas_call(
        pack_kernel,
        out_shape=jax.ShapeDtypeStruct((TILES, 16, 128), BF),
        in_specs=[ANY] * 5,
        out_specs=vmem(1)[0],
        scratch_shapes=[pltpu.VMEM(a.shape, BF) for a in shards] + [pltpu.SemaphoreType.DMA((5,))],
        compiler_params=small(60),
        name="pack",
    )(*shards)
    along_z = lax.all_to_all(
        jnp.broadcast_to(packed[None], (NZ, TILES, 16, 128)),
        "seq",
        0,
        0,
        axis_index_groups=Z_GROUPS,
        tiled=True,
    )
    first = ring(along_z[:, :GROUP], 0)
    own_s = ring_by_halves(reorder(halves_kernel, [along_z] + first[1:], [20, 20], "halves"), 1)
    oth_s = [swap(b) for b in own_s]
    (part_t,) = reorder(temporal_blocks_kernel, own_s, [32], "temporal_blocks")
    ring_t = ring(part_t, 0)

    hidden, tnormed = call(
        spatial_kernel,
        own_s + oth_s + [latents, gain_s, gain_t],
        [(PIX, D), (PIX, 5, 2, 128)],
        [
            (NX, NZ, NY, 16, 256),
            (1920, 256),
            (GROUP, 1024, 128),
            (INNER, 128),
            (NX, NZ, NY, 48, 128),
            (D, 128),
        ],
        "spatial",
        9 * 10**9,
        24,
    )
    tokens = lax.all_to_all(tnormed, "seq", 0, 0, tiled=True)
    own_t = ring_t[:1] + gate(ring_t[1:], tokens)
    oth_t = [swap(ring_t[0])] + [swap(b) for b in own_t[1:]]
    tattn = call(
        temporal_kernel,
        own_t + oth_t + [tokens],
        [(PIX, 3, 2, 128)],
        [(NX, NZ, NY, 16, 128), (1920, 128), (INNER, 128), (D, 128), (768, 128)],
        "temporal",
        5 * 10**9,
        16,
    )
    back = lax.all_to_all(tattn, "seq", 0, 0, tiled=True)
    mixed = call(
        mixed_kernel,
        own_t + oth_t + [back, hidden],
        [(PIX, D)],
        [(NX, NZ, NY, 48, 128), (D, 128), (768, 128)],
        "mixed",
        3 * 10**9,
        16,
    )
    return mixed.reshape(1, PIX, D)


def solution(mesh):
    in_specs = (
        P(("clip", "seq"), None, None),
        P(("clip", "seq"), None),
        P(),
        P(None, "seq"),
        P(None, "seq"),
        P(),
        P(None, "seq"),
        P(None, "seq"),
    )
    out_specs = P(("clip", "seq"), None, None)
    return jax.shard_map(body, mesh=mesh, in_specs=in_specs, out_specs=out_specs, check_vma=False)
```

```python
import functools
import itertools

import jax
import jax.numpy as jnp
from jax import lax
from jax.experimental import pallas as pl
from jax.experimental.pallas import tpu as pltpu
from jax.sharding import PartitionSpec as P

D = 1280
HEADS = 10
HEAD = 64
INNER = 640
PIX = 128
NX, NZ, NY = 4, 8, 4
SEQ = NX * NZ * NY
EPS = 1e-05
BF = jnp.bfloat16
F32 = jnp.float32
SHIFTS = (0, 1, 3, 2)
GROUP = 7
TILES = 2 * GROUP


def seq_of(x, z, y):
    return (x * NZ + z) * NY + y


Z_GROUPS = [[seq_of(x, z, y) for z in range(NZ)] for x in range(NX) for y in range(NY)]
SWAP = [(i, (i + SEQ) % (2 * SEQ)) for i in range(2 * SEQ)]


def ring_perm(k, stage):
    pairs = []
    for c, x, z, y in itertools.product(range(2), range(NX), range(NZ), range(NY)):
        if (c + stage) % 2 == 0:
            to = ((x + k) % NX, z, y)
        else:
            to = (x, z, (y + k) % NY)
        pairs.append((c * SEQ + seq_of(x, z, y), c * SEQ + seq_of(*to)))
    return pairs


def ring(block, stage):
    return [block] + [
        lax.ppermute(block, ("clip", "seq"), ring_perm(k, stage)) for k in SHIFTS[1:]
    ]


def ring_by_halves(pair, stage):
    def shift(part, k):
        return lax.ppermute(part, ("clip", "seq"), ring_perm(k, stage))

    one, two = pair
    up_one, down_two = shift(one, 1), shift(two, 3)
    up_two, down_one = shift(two, 1), shift(one, 3)
    far_one, far_two = shift(up_one, 1), shift(down_two, 3)
    return [one, two, up_one, up_two, down_one, down_two, far_one, far_two]


def swap(block):
    return lax.ppermute(block, ("clip", "seq"), SWAP)


def vmem(n):
    return [pl.BlockSpec(memory_space=pltpu.VMEM)] * n


ANY = pl.BlockSpec(memory_space=pl.ANY)


def small(mib):
    return pltpu.CompilerParams(vmem_limit_bytes=mib * 1024 * 1024)


def layer_norm(x, gain):
    mean = jnp.mean(x, axis=-1, keepdims=True)
    d = x - mean
    var = jnp.mean(d * d, axis=-1, keepdims=True)
    return (d * lax.rsqrt(var + EPS) * gain).astype(BF)


def pack_kernel(ws_in, ref_in, wo_in, wt_in, wu_in, out, ws, ref, wo, wt, wu, sems):
    c = lax.axis_index("clip")
    pairs = ((ws_in, ws), (ref_in, ref), (wo_in, wo), (wt_in, wt), (wu_in, wu))
    copies = [pltpu.make_async_copy(src, dst, sems.at[i]) for i, (src, dst) in enumerate(pairs)]
    for copy in copies:
        copy.start()
    for copy in copies:
        copy.wait()

    def tile(*rows):
        n = sum(r.shape[0] for r in rows)
        parts = [r.astype(F32) for r in rows]
        if n < 16:
            parts.append(jnp.zeros((16 - n, 128), F32))
        return jnp.concatenate(parts, axis=0).astype(BF)

    def lane(ref, t):
        return ref[:, 128 * t : 128 * (t + 1)]

    def fill(half):
        refs = [lane(ref, u) for u in range(10)]
        def put(at, value):
            for z in range(NZ):
                out[z, at] = value

        for t in range(5):
            put(t, tile(lane(ws, 5 * half + t), refs[t]))
            put(GROUP + t, tile(lane(wt, 5 * half + t)))
        for at, w, extra in ((5, wo, refs[5:]), (GROUP + 5, wu, [])):
            middle = lane(w, 2).astype(F32)[5 * half : 5 * half + 5]
            put(at, tile(lane(w, 3 * half), middle))
            put(at + 1, tile(lane(w, 3 * half + 1), *extra))

    for half in range(2):
        pl.when(c == half)(functools.partial(fill, half))


def halves_kernel(along_z, p1, p2, p3, one, two):
    spatial = (along_z, p1, p2, p3)
    for half, out in enumerate((one, two)):
        for i in range(2):
            out[8 * i : 8 * i + 8] = spatial[2 * half + i][:, 0:GROUP]
        out[16:20] = along_z[4 * half : 4 * half + 4, GROUP : 2 * GROUP]


def temporal_blocks_kernel(*refs):
    out = refs[-1]
    for i, piece in enumerate(refs[:-1]):
        out[4 * i : 4 * i + 4] = piece[16:20]


def gate_kernel(*refs):
    pass


def gate(values, after):
    n = len(values)
    return list(
        pl.pallas_call(
            gate_kernel,
            out_shape=[jax.ShapeDtypeStruct(v.shape, v.dtype) for v in values],
            in_specs=vmem(n + 1),
            out_specs=vmem(n),
            input_output_aliases={i: i for i in range(n)},
            compiler_params=small(4),
            name="gate",
        )(*values, after)
    )


def reorder(kernel, args, outs, name):
    return pl.pallas_call(
        kernel,
        out_shape=[jax.ShapeDtypeStruct(n + (16, 128), BF) for n in outs],
        in_specs=vmem(len(args)),
        out_specs=vmem(len(outs)),
        compiler_params=small(8),
        name=name,
    )(*args)


def to_rows(value, out, rows, n):
    wide = 2 * out.shape[1]
    for t in range(wide):
        at = pl.ds(t, 128, stride=wide)
        rows[at, :] = value[:, 128 * t : 128 * (t + 1)] if t < n else jnp.zeros((128, 128), F32)
    out.reshape(128 * wide, 128)[...] = rows[...].astype(BF)


def from_rows(ref, rows, n):
    wide = 2 * ref.shape[1]
    rows[...] = ref.reshape(128 * wide, 128)[...].astype(F32)
    return jnp.concatenate(
        [rows[pl.ds(t, 128, stride=wide), :] for t in range(n)], axis=1
    ).astype(BF)


def place():
    s = lax.axis_index("seq")
    return lax.axis_index("clip"), s // (NZ * NY), lax.rem(s, NY)


def blocks(refs, j, i):
    each = 16 // len(refs)
    at = 4 * j + i
    return refs[at // each], 8 * (at % each)


def lanes(refs, j, i, first, count):
    ref, start = blocks(refs, j, i)
    parts = [ref[start : start + 8, first + t].reshape(128, 128) for t in range(count)]
    return jnp.concatenate(parts, axis=1)


def pieces_of(own, oth, j, first, count):
    wa = [lanes(own, j, i, first, count) for i in range(4)]
    wb = [lanes(oth, i, j, first, count) for i in range(4)]
    return jnp.concatenate(wa, axis=0), jnp.concatenate(wb, axis=0)


def spread(acc, r, j, row, x_core):
    c, x, y = place()
    for i in range(4):
        dx = jnp.where(c == x_core, SHIFTS[i], SHIFTS[j])
        dy = jnp.where(c == x_core, SHIFTS[j], SHIFTS[i])
        xs = lax.rem(x - dx + NX, NX)
        ys = lax.rem(y - dy + NY, NY)
        for z in range(NZ):
            at = (i * 8 + z) * 16
            acc[xs, z, ys, row : row + 16, :] = r[at : at + 16]


NT = (((1,), (1,)), ((), ()))
NN = (((1,), (0,)), ((), ()))


def dot(a, b, dims):
    return lax.dot_general(a, b, dims, preferred_element_type=F32)


def compact(acc, rows):
    for s in range(SEQ):
        x, z, y = s // 32, (s // 4) % 8, s % 4
        rows[15 * s : 15 * s + 15, :] = acc[x, z, y, 0:15, :]


def qkv_project(own, oth, acc, rows, tokens, x_core):
    c, _, _ = place()
    xa, xb = halves(tokens, c)
    for j in range(4):
        wa, wb = pieces_of(own, oth, j, 0, 5)
        spread(acc, dot(wa, xa, NT) + dot(wb, xb, NT), j, 0, x_core)
    compact(acc, rows)


def out_project(own, oth, acc, rows, part, dims, x_core):
    c, _, _ = place()
    lo, mid, hi = part(0, 256), part(256, 384), part(384, 640)
    xa = jnp.where(c == 0, lo, hi)
    xb = jnp.where(c == 0, hi, lo)
    for j in range(4):
        wa, wb = pieces_of(own, oth, j, 5, 2)
        spread(acc, dot(wa, xa, dims) + dot(wb, xb, dims), j, 0, x_core)
        ma, mb = dot(wa[:, :128], mid, dims), dot(wb[:, :128], mid, dims)
        spread(acc, jnp.where(c == 0, ma, mb), j, 16, x_core)
        spread(acc, jnp.where(c == 0, mb, ma), j, 32, x_core)
    for s in range(SEQ):
        x, z, y = s // 32, (s // 4) % 8, s % 4
        m0 = acc[x, z, y, 26:31, :]
        m1 = acc[x, z, y, 42:47, :]
        rows[10 * s : 10 * s + 10, :] = acc[x, z, y, 0:10, :] + jnp.concatenate([m0, m1], axis=0)


def halves(xv, c):
    lo, hi = xv[:, :640], xv[:, 640:]
    first = c == 0
    return jnp.where(first, lo, hi), jnp.where(first, hi, lo)


def heads(rows, keys, attn):
    for h in range(HEADS):
        q = rows[64 * h : 64 * (h + 1), 0:128].astype(BF)
        k = rows[640 + 64 * h : 640 + 64 * (h + 1), 0:keys].astype(BF)
        v = rows[1280 + 64 * h : 1280 + 64 * (h + 1), 0:keys].astype(BF)
        st = lax.dot_general(k, q, (((0,), (0,)), ((), ())), preferred_element_type=F32)
        st = st * (HEAD**-0.5)
        e = jnp.exp(st - jnp.max(st, axis=0, keepdims=True))
        p = (e * (1.0 / jnp.sum(e, axis=0, keepdims=True))).astype(BF)
        attn[64 * h : 64 * (h + 1), :] = jnp.dot(v, p, preferred_element_type=F32)


def reference_tokens(own, last):
    parts = []
    for t in (0, 1, 2, 3, 4, 6):
        for j in range(4):
            for i in range(4):
                at = (j * 4 + i) * 64
                ref, start = blocks(own, j, i)
                tail = ref[start : start + 8, t].astype(F32)[:, 8:16, :]
                last[t, at : at + 64, :] = tail.reshape(64, 128)
        at = (7,) if t < 5 else (2, 3, 4, 5, 6)
        parts += [last[t, pl.ds(r, 128, stride=8), :] for r in at]
    return jnp.concatenate(parts, axis=1).astype(BF)


def spatial_kernel(*refs):
    own, oth = refs[0:8], refs[8:16]
    latents, gain_s, gain_t, hidden, tnormed, acc, rows, last, attn, acc_out, rows_out = refs[16:]
    normed = layer_norm(latents[...].astype(F32), gain_s[...])
    tokens = jnp.concatenate([normed, reference_tokens(own, last)], axis=0)
    qkv_project(own, oth, acc, rows, tokens, 0)
    heads(rows, 256, attn)
    part = lambda a, b: attn[a:b, :].astype(BF)
    out_project(own, oth, acc_out, rows_out, part, NN, 0)
    h = (latents[...].astype(F32) + rows_out[...].T).astype(BF)
    hidden[...] = h
    to_rows(layer_norm(h.astype(F32), gain_t[...]).astype(F32), tnormed, rows_out, 10)


def half_kernel(*refs):
    own, (tokens, out, for_out, wide) = refs[0:4], refs[4:]
    c, _, _ = place()
    xa, _ = halves(from_rows(tokens, wide, 10), c)
    for j in range(4):
        wa = jnp.concatenate([lanes(own, j, i, 0, 5) for i in range(4)], axis=0)
        out[512 * j : 512 * (j + 1), :] = dot(wa, xa, NT)
        for_out[32 * j : 32 * (j + 1)] = own[j][:, 5:7]


def temporal_kernel(*refs):
    oth = refs[0:4]
    half, tokens, out, for_out, acc, rows, attn, wide, wide_out = refs[4:]
    c, _, _ = place()
    _, xb = halves(from_rows(tokens, wide, 10), c)
    for j in range(4):
        wb = jnp.concatenate([lanes(oth, i, j, 0, 5) for i in range(4)], axis=0)
        spread(acc, half[512 * j : 512 * (j + 1), :] + dot(wb, xb, NT), j, 0, 1)
        for_out[32 * j : 32 * (j + 1)] = oth[j][:, 5:7]
    compact(acc, rows)
    heads(rows, 128, attn)
    to_rows(attn[...].T, out, wide_out, 5)


def weights_kernel(*refs):
    own, oth, out, acc, rows = refs
    c, _, _ = place()
    for j in range(4):
        wa, wb = pieces_of([own], [oth], j, 0, 2)
        lo = jnp.where(c == 0, wa, wb).astype(F32)
        hi = jnp.where(c == 0, wb, wa).astype(F32)
        spread(acc, jnp.concatenate([lo, hi], axis=1), j, 0, 1)
    for s in range(SEQ):
        x, z, y = s // 32, (s // 4) % 8, s % 4
        at = slice(10 * s, 10 * s + 10)
        rows[at, 0:256] = acc[x, z, y, 0:10, 0:256]
        rows[at, 384:640] = acc[x, z, y, 0:10, 256:512]
        rows[at, 256:384] = jnp.concatenate(
            [acc[x, z, y, 10:15, 0:128], acc[x, z, y, 10:15, 256:384]], axis=0
        )
    out[...] = rows[...].astype(BF)


def mixed_kernel(weights, attn, hidden, mixed, wide):
    a = from_rows(attn, wide, 5)
    mixed[...] = (hidden[...].astype(F32) + dot(a, weights[...], NT)).astype(BF)


def call(kernel, args, outs, scratch, name, flops, mib, dtypes=(BF, BF)):
    shapes = [jax.ShapeDtypeStruct(s, d) for s, d in zip(outs, dtypes)]
    single = len(shapes) == 1
    size = sum(a.size * a.dtype.itemsize for a in args) + sum(2 * s.size for s in shapes)
    return pl.pallas_call(
        kernel,
        out_shape=shapes[0] if single else shapes,
        in_specs=vmem(len(args)),
        out_specs=vmem(1)[0] if single else vmem(len(shapes)),
        scratch_shapes=[pltpu.VMEM(s, F32) for s in scratch],
        compiler_params=small(mib),
        cost_estimate=pl.CostEstimate(flops=flops, bytes_accessed=size, transcendentals=0),
        name=name,
    )(*args)


def body(latents, ref_hidden, gain_s, w_s, w_o, gain_t, w_t, w_u):
    latents = latents.reshape(PIX, D)
    gain_s = gain_s.reshape(1, D)
    gain_t = gain_t.reshape(1, D)
    shards = [w_s.T, ref_hidden, w_o.T, w_t.T, w_u.T]
    packed = pl.pallas_call(
        pack_kernel,
        out_shape=jax.ShapeDtypeStruct((NZ, TILES, 16, 128), BF),
        in_specs=[ANY] * 5,
        out_specs=vmem(1)[0],
        scratch_shapes=[pltpu.VMEM(a.shape, BF) for a in shards] + [pltpu.SemaphoreType.DMA((5,))],
        compiler_params=small(60),
        name="pack",
    )(*shards)
    along_z = lax.all_to_all(
        packed,
        "seq",
        0,
        0,
        axis_index_groups=Z_GROUPS,
        tiled=True,
    )
    first = ring(along_z[:, :GROUP], 0)
    own_s = ring_by_halves(reorder(halves_kernel, [along_z] + first[1:], [(20, GROUP)] * 2, "halves"), 1)
    oth_s = [swap(b) for b in own_s]
    (part_t,) = reorder(temporal_blocks_kernel, own_s, [(32, GROUP)], "temporal_blocks")
    ring_t = ring(part_t, 0)

    hidden, tnormed = call(
        spatial_kernel,
        own_s + oth_s + [latents, gain_s, gain_t],
        [(PIX, D), (PIX, 5, 2, 128)],
        [
            (NX, NZ, NY, 16, 256),
            (1920, 256),
            (GROUP, 1024, 128),
            (INNER, 128),
            (NX, NZ, NY, 48, 128),
            (D, 128),
        ],
        "spatial",
        9 * 10**9,
        32,
    )
    tokens = lax.all_to_all(tnormed, "seq", 0, 0, tiled=True)
    own_t = ring_t[:1] + gate(ring_t[1:], tokens)
    oth_t = [swap(ring_t[0])] + [swap(b) for b in own_t[1:]]
    half_t, own_u = call(
        half_kernel,
        own_t + [tokens],
        [(2048, 128), (SEQ, 2, 16, 128)],
        [(D, 128)],
        "half",
        3 * 10**9,
        16,
        [F32, BF],
    )
    tattn, oth_u = call(
        temporal_kernel,
        oth_t + [half_t, tokens],
        [(PIX, 3, 2, 128), (SEQ, 2, 16, 128)],
        [(NX, NZ, NY, 16, 128), (1920, 128), (INNER, 128), (D, 128), (768, 128)],
        "temporal",
        5 * 10**9,
        16,
    )
    weights_u = call(
        weights_kernel,
        [own_u, oth_u],
        [(D, INNER)],
        [(NX, NZ, NY, 16, 512), (D, INNER)],
        "weights",
        3 * 10**9,
        16,
    )
    back = lax.all_to_all(tattn, "seq", 0, 0, tiled=True)
    mixed = call(
        mixed_kernel,
        [weights_u, back, hidden],
        [(PIX, D)],
        [(768, 128)],
        "mixed",
        10**9,
        8,
    )
    return mixed.reshape(1, PIX, D)


def solution(mesh):
    in_specs = (
        P(("clip", "seq"), None, None),
        P(("clip", "seq"), None),
        P(),
        P(None, "seq"),
        P(None, "seq"),
        P(),
        P(None, "seq"),
        P(None, "seq"),
    )
    out_specs = P(("clip", "seq"), None, None)
    return jax.shard_map(body, mesh=mesh, in_specs=in_specs, out_specs=out_specs, check_vma=False)
```

```python
import functools
import itertools

import jax
import jax.numpy as jnp
from jax import lax
from jax.experimental import pallas as pl
from jax.experimental.pallas import tpu as pltpu
from jax.sharding import PartitionSpec as P

D = 1280
HEADS = 10
HEAD = 64
INNER = 640
PIX = 128
NX, NZ, NY = 4, 8, 4
SEQ = NX * NZ * NY
EPS = 1e-05
BF = jnp.bfloat16
F32 = jnp.float32
SHIFTS = (0, 1, 3, 2)
GROUP = 7
TILES = 2 * GROUP


def seq_of(x, z, y):
    return (x * NZ + z) * NY + y


Z_GROUPS = [[seq_of(x, z, y) for z in range(NZ)] for x in range(NX) for y in range(NY)]
SWAP = [(i, (i + SEQ) % (2 * SEQ)) for i in range(2 * SEQ)]


def ring_perm(k, stage):
    pairs = []
    for c, x, z, y in itertools.product(range(2), range(NX), range(NZ), range(NY)):
        if (c + stage) % 2 == 0:
            to = ((x + k) % NX, z, y)
        else:
            to = (x, z, (y + k) % NY)
        pairs.append((c * SEQ + seq_of(x, z, y), c * SEQ + seq_of(*to)))
    return pairs


def ring(block, stage):
    return [block] + [
        lax.ppermute(block, ("clip", "seq"), ring_perm(k, stage)) for k in SHIFTS[1:]
    ]


def ring_by_halves(pair, stage):
    def shift(part, k):
        return lax.ppermute(part, ("clip", "seq"), ring_perm(k, stage))

    one, two = pair
    up_one, down_two = shift(one, 1), shift(two, 3)
    up_two, down_one = shift(two, 1), shift(one, 3)
    far_one, far_two = shift(up_one, 1), shift(down_two, 3)
    return [one, two, up_one, up_two, down_one, down_two, far_one, far_two]


def swap(block):
    return lax.ppermute(block, ("clip", "seq"), SWAP)


def vmem(n):
    return [pl.BlockSpec(memory_space=pltpu.VMEM)] * n


ANY = pl.BlockSpec(memory_space=pl.ANY)
HBM = pl.BlockSpec(memory_space=pltpu.HBM)


def small(mib):
    return pltpu.CompilerParams(vmem_limit_bytes=mib * 1024 * 1024)


def layer_norm(x, gain):
    mean = jnp.mean(x, axis=-1, keepdims=True)
    d = x - mean
    var = jnp.mean(d * d, axis=-1, keepdims=True)
    return (d * lax.rsqrt(var + EPS) * gain).astype(BF)


def pack_kernel(ws_in, ref_in, wo_in, wt_in, wu_in, out, ws, ref, wo, wt, wu, sems):
    c = lax.axis_index("clip")
    pairs = ((ws_in, ws), (ref_in, ref), (wo_in, wo), (wt_in, wt), (wu_in, wu))
    copies = [pltpu.make_async_copy(src, dst, sems.at[i]) for i, (src, dst) in enumerate(pairs)]
    for copy in copies:
        copy.start()
    for copy in copies:
        copy.wait()

    def tile(*rows):
        n = sum(r.shape[0] for r in rows)
        parts = [r.astype(F32) for r in rows]
        if n < 16:
            parts.append(jnp.zeros((16 - n, 128), F32))
        return jnp.concatenate(parts, axis=0).astype(BF)

    def lane(ref, t):
        return ref[:, 128 * t : 128 * (t + 1)]

    def fill(half):
        refs = [lane(ref, u) for u in range(10)]
        def put(at, value):
            for z in range(NZ):
                out[z, at] = value

        for t in range(5):
            put(t, tile(lane(ws, 5 * half + t), refs[t]))
            put(GROUP + t, tile(lane(wt, 5 * half + t)))
        for at, w, extra in ((5, wo, refs[5:]), (GROUP + 5, wu, [])):
            middle = lane(w, 2).astype(F32)[5 * half : 5 * half + 5]
            put(at, tile(lane(w, 3 * half), middle))
            put(at + 1, tile(lane(w, 3 * half + 1), *extra))

    for half in range(2):
        pl.when(c == half)(functools.partial(fill, half))


def halves_kernel(along_z, p1, p2, p3, one, two):
    spatial = (along_z, p1, p2, p3)
    for half, out in enumerate((one, two)):
        for i in range(2):
            out[8 * i : 8 * i + 8] = spatial[2 * half + i][:, 0:GROUP]
        out[16:20] = along_z[4 * half : 4 * half + 4, GROUP : 2 * GROUP]


def temporal_blocks_kernel(*refs):
    out = refs[-1]
    for i, piece in enumerate(refs[:-1]):
        out[4 * i : 4 * i + 4] = piece[16:20]


def gate_kernel(*refs):
    pass


def gate(values, after):
    n = len(values)
    return list(
        pl.pallas_call(
            gate_kernel,
            out_shape=[jax.ShapeDtypeStruct(v.shape, v.dtype) for v in values],
            in_specs=vmem(n + 1),
            out_specs=vmem(n),
            input_output_aliases={i: i for i in range(n)},
            compiler_params=small(4),
            name="gate",
        )(*values, after)
    )


def reorder(kernel, args, outs, name):
    return pl.pallas_call(
        kernel,
        out_shape=[jax.ShapeDtypeStruct(n + (16, 128), BF) for n in outs],
        in_specs=vmem(len(args)),
        out_specs=vmem(len(outs)),
        compiler_params=small(8),
        name=name,
    )(*args)


def to_rows(value, out, rows, n):
    wide = 2 * out.shape[1]
    for t in range(wide):
        at = pl.ds(t, 128, stride=wide)
        rows[at, :] = value[:, 128 * t : 128 * (t + 1)] if t < n else jnp.zeros((128, 128), F32)
    out.reshape(128 * wide, 128)[...] = rows[...].astype(BF)


def from_rows(ref, rows, n):
    wide = 2 * ref.shape[1]
    rows[...] = ref.reshape(128 * wide, 128)[...].astype(F32)
    return jnp.concatenate(
        [rows[pl.ds(t, 128, stride=wide), :] for t in range(n)], axis=1
    ).astype(BF)


def place():
    s = lax.axis_index("seq")
    return lax.axis_index("clip"), s // (NZ * NY), lax.rem(s, NY)


def blocks(refs, j, i):
    each = 16 // len(refs)
    at = 4 * j + i
    return refs[at // each], 8 * (at % each)


def lanes(refs, j, i, first, count):
    ref, start = blocks(refs, j, i)
    parts = [ref[start : start + 8, first + t].reshape(128, 128) for t in range(count)]
    return jnp.concatenate(parts, axis=1)


def pieces_of(own, oth, j, first, count):
    wa = [lanes(own, j, i, first, count) for i in range(4)]
    wb = [lanes(oth, i, j, first, count) for i in range(4)]
    return jnp.concatenate(wa, axis=0), jnp.concatenate(wb, axis=0)


def spread(acc, r, j, row, x_core):
    c, x, y = place()
    for i in range(4):
        dx = jnp.where(c == x_core, SHIFTS[i], SHIFTS[j])
        dy = jnp.where(c == x_core, SHIFTS[j], SHIFTS[i])
        xs = lax.rem(x - dx + NX, NX)
        ys = lax.rem(y - dy + NY, NY)
        for z in range(NZ):
            at = (i * 8 + z) * 16
            acc[xs, z, ys, row : row + 16, :] = r[at : at + 16]


NT = (((1,), (1,)), ((), ()))
NN = (((1,), (0,)), ((), ()))


def dot(a, b, dims):
    return lax.dot_general(a, b, dims, preferred_element_type=F32)


def compact(acc, rows):
    for s in range(SEQ):
        x, z, y = s // 32, (s // 4) % 8, s % 4
        rows[15 * s : 15 * s + 15, :] = acc[x, z, y, 0:15, :]


def qkv_project(own, oth, acc, rows, tokens, x_core):
    c, _, _ = place()
    xa, xb = halves(tokens, c)
    for j in range(4):
        wa, wb = pieces_of(own, oth, j, 0, 5)
        spread(acc, dot(wa, xa, NT) + dot(wb, xb, NT), j, 0, x_core)
    compact(acc, rows)


def out_project(own, oth, acc, rows, part, dims, x_core):
    c, _, _ = place()
    lo, mid, hi = part(0, 256), part(256, 384), part(384, 640)
    upper = lax.rem(lax.broadcasted_iota(jnp.int32, (512, 128), 0), 16) < 10
    xa = jnp.where(c == 0, lo, hi)
    xb = jnp.where(c == 0, hi, lo)
    for j in range(4):
        wa, wb = pieces_of(own, oth, j, 5, 2)
        both = dot(wa, xa, dims) + dot(wb, xb, dims)
        ma, mb = dot(wa[:, :128], mid, dims), dot(wb[:, :128], mid, dims)
        m0, m1 = jnp.where(c == 0, ma, mb), jnp.where(c == 0, mb, ma)
        spread(acc, jnp.where(upper, both, m0), j, 0, x_core)
        spread(acc, m1, j, 16, x_core)
    for s in range(SEQ):
        x, z, y = s // 32, (s // 4) % 8, s % 4
        m0 = acc[x, z, y, 10:15, :]
        m1 = acc[x, z, y, 26:31, :]
        rows[10 * s : 10 * s + 10, :] = acc[x, z, y, 0:10, :] + jnp.concatenate([m0, m1], axis=0)


def halves(xv, c):
    lo, hi = xv[:, :640], xv[:, 640:]
    first = c == 0
    return jnp.where(first, lo, hi), jnp.where(first, hi, lo)


def heads(rows, scores, attn):
    keys = scores.shape[1]
    for h in range(HEADS):
        q = rows[64 * h : 64 * (h + 1), 0:128].astype(BF)
        k = rows[640 + 64 * h : 640 + 64 * (h + 1), 0:keys].astype(BF)
        scores[h] = dot(k, q, (((0,), (0,)), ((), ())))
    for h in range(HEADS):
        st = scores[h] * (HEAD**-0.5)
        e = jnp.exp(st - jnp.max(st, axis=0, keepdims=True))
        p = (e * (1.0 / jnp.sum(e, axis=0, keepdims=True))).astype(BF)
        v = rows[1280 + 64 * h : 1280 + 64 * (h + 1), 0:keys].astype(BF)
        attn[64 * h : 64 * (h + 1), :] = dot(v, p, NN)


def reference_tokens(own, last):
    parts = []
    for t in (0, 1, 2, 3, 4, 6):
        for j in range(4):
            for i in range(4):
                at = (j * 4 + i) * 64
                ref, start = blocks(own, j, i)
                tail = ref[start : start + 8, t].astype(F32)[:, 8:16, :]
                last[t, at : at + 64, :] = tail.reshape(64, 128)
        at = (7,) if t < 5 else (2, 3, 4, 5, 6)
        parts += [last[t, pl.ds(r, 128, stride=8), :] for r in at]
    return jnp.concatenate(parts, axis=1).astype(BF)


def spatial_kernel(*refs):
    own, oth = refs[0:8], refs[8:16]
    latents, gain_s, gain_t, hidden, tnormed, acc, rows, last, attn, scores, acc_out, rows_out = refs[16:]
    normed = layer_norm(latents[...].astype(F32), gain_s[...])
    tokens = jnp.concatenate([normed, reference_tokens(own, last)], axis=0)
    qkv_project(own, oth, acc, rows, tokens, 0)
    heads(rows, scores, attn)
    part = lambda a, b: attn[a:b, :].astype(BF)
    out_project(own, oth, acc_out, rows_out, part, NN, 0)
    h = (latents[...].astype(F32) + rows_out[...].T).astype(BF)
    hidden[...] = h
    to_rows(layer_norm(h.astype(F32), gain_t[...]).astype(F32), tnormed, rows_out, 10)


def output_tiles(pieces, out, sems):
    copies = [
        pltpu.make_async_copy(p.at[:, pl.ds(5, 2)], out.at[pl.ds(32 * j, 32)], sems.at[j])
        for j, p in enumerate(pieces)
    ]
    for copy in copies:
        copy.start()
    return copies


def half_kernel(*refs):
    own, (tokens, out, for_out, wide, sems) = refs[0:4], refs[4:]
    c, _, _ = place()
    copies = output_tiles(own, for_out, sems)
    xa, _ = halves(from_rows(tokens, wide, 10), c)
    for j in range(4):
        wa = jnp.concatenate([lanes(own, j, i, 0, 5) for i in range(4)], axis=0)
        out[512 * j : 512 * (j + 1), :] = dot(wa, xa, NT)
    for copy in copies:
        copy.wait()


def temporal_kernel(*refs):
    oth = refs[0:4]
    half, tokens, out, for_out, acc, rows, attn, scores, wide, wide_out, sems = refs[4:]
    c, _, _ = place()
    copies = output_tiles(oth, for_out, sems)
    _, xb = halves(from_rows(tokens, wide, 10), c)
    for j in range(4):
        wb = jnp.concatenate([lanes(oth, i, j, 0, 5) for i in range(4)], axis=0)
        spread(acc, half[512 * j : 512 * (j + 1), :] + dot(wb, xb, NT), j, 0, 1)
    compact(acc, rows)
    heads(rows, scores, attn)
    to_rows(attn[...].T, out, wide_out, 5)
    for copy in copies:
        copy.wait()


def weights_kernel(*refs):
    own, oth, out, acc, rows = refs
    c, _, _ = place()
    for j in range(4):
        wa, wb = pieces_of([own], [oth], j, 0, 2)
        lo = jnp.where(c == 0, wa, wb).astype(F32)
        hi = jnp.where(c == 0, wb, wa).astype(F32)
        spread(acc, jnp.concatenate([lo, hi], axis=1), j, 0, 1)
    for s in range(SEQ):
        x, z, y = s // 32, (s // 4) % 8, s % 4
        at = slice(10 * s, 10 * s + 10)
        rows[at, 0:256] = acc[x, z, y, 0:10, 0:256]
        rows[at, 384:640] = acc[x, z, y, 0:10, 256:512]
        rows[at, 256:384] = jnp.concatenate(
            [acc[x, z, y, 10:15, 0:128], acc[x, z, y, 10:15, 256:384]], axis=0
        )
    out[...] = rows[...].astype(BF)


def mixed_kernel(weights, attn, hidden, mixed, wide):
    a = from_rows(attn, wide, 5)
    mixed[...] = (hidden[...].astype(F32) + dot(a, weights[...], NT)).astype(BF)


def call(kernel, args, outs, scratch, name, flops, mib, dtypes=(BF, BF)):
    shapes = [jax.ShapeDtypeStruct(s, d) for s, d in zip(outs, dtypes)]
    single = len(shapes) == 1
    size = sum(a.size * a.dtype.itemsize for a in args) + sum(2 * s.size for s in shapes)
    return pl.pallas_call(
        kernel,
        out_shape=shapes[0] if single else shapes,
        in_specs=vmem(len(args)),
        out_specs=vmem(1)[0] if single else [HBM if s == (SEQ, 2, 16, 128) else vmem(1)[0] for s in outs],
        scratch_shapes=[pltpu.VMEM(s, F32) if isinstance(s, tuple) else s for s in scratch],
        compiler_params=small(mib),
        cost_estimate=pl.CostEstimate(flops=flops, bytes_accessed=size, transcendentals=0),
        name=name,
    )(*args)


def body(latents, ref_hidden, gain_s, w_s, w_o, gain_t, w_t, w_u):
    latents = latents.reshape(PIX, D)
    gain_s = gain_s.reshape(1, D)
    gain_t = gain_t.reshape(1, D)
    shards = [w_s.T, ref_hidden, w_o.T, w_t.T, w_u.T]
    packed = pl.pallas_call(
        pack_kernel,
        out_shape=jax.ShapeDtypeStruct((NZ, TILES, 16, 128), BF),
        in_specs=[ANY] * 5,
        out_specs=vmem(1)[0],
        scratch_shapes=[pltpu.VMEM(a.shape, BF) for a in shards] + [pltpu.SemaphoreType.DMA((5,))],
        compiler_params=small(60),
        name="pack",
    )(*shards)
    along_z = lax.all_to_all(
        packed,
        "seq",
        0,
        0,
        axis_index_groups=Z_GROUPS,
        tiled=True,
    )
    first = ring(along_z[:, :GROUP], 0)
    own_s = ring_by_halves(reorder(halves_kernel, [along_z] + first[1:], [(20, GROUP)] * 2, "halves"), 1)
    oth_s = [swap(b) for b in own_s]
    (part_t,) = reorder(temporal_blocks_kernel, own_s, [(32, GROUP)], "temporal_blocks")
    ring_t = ring(part_t, 0)

    hidden, tnormed = call(
        spatial_kernel,
        own_s + oth_s + [latents, gain_s, gain_t],
        [(PIX, D), (PIX, 5, 2, 128)],
        [
            (NX, NZ, NY, 16, 256),
            (1920, 256),
            (GROUP, 1024, 128),
            (INNER, 128),
            (HEADS, 256, 128),
            (NX, NZ, NY, 32, 128),
            (D, 128),
        ],
        "spatial",
        9 * 10**9,
        32,
    )
    tokens = lax.all_to_all(tnormed, "seq", 0, 0, tiled=True)
    own_t = ring_t[:1] + gate(ring_t[1:], tokens)
    oth_t = [swap(ring_t[0])] + [swap(b) for b in own_t[1:]]
    half_t, own_u = call(
        half_kernel,
        own_t + [tokens],
        [(2048, 128), (SEQ, 2, 16, 128)],
        [(D, 128), pltpu.SemaphoreType.DMA((4,))],
        "half",
        3 * 10**9,
        16,
        [F32, BF],
    )
    tattn, oth_u = call(
        temporal_kernel,
        oth_t + [half_t, tokens],
        [(PIX, 3, 2, 128), (SEQ, 2, 16, 128)],
        [
            (NX, NZ, NY, 16, 128),
            (1920, 128),
            (INNER, 128),
            (HEADS, 128, 128),
            (D, 128),
            (768, 128),
            pltpu.SemaphoreType.DMA((4,)),
        ],
        "temporal",
        5 * 10**9,
        16,
    )
    weights_u = call(
        weights_kernel,
        [own_u, oth_u],
        [(D, INNER)],
        [(NX, NZ, NY, 16, 512), (D, INNER)],
        "weights",
        3 * 10**9,
        16,
    )
    back = lax.all_to_all(tattn, "seq", 0, 0, tiled=True)
    mixed = call(
        mixed_kernel,
        [weights_u, back, hidden],
        [(PIX, D)],
        [(768, 128)],
        "mixed",
        10**9,
        8,
    )
    return mixed.reshape(1, PIX, D)


def solution(mesh):
    in_specs = (
        P(("clip", "seq"), None, None),
        P(("clip", "seq"), None),
        P(),
        P(None, "seq"),
        P(None, "seq"),
        P(),
        P(None, "seq"),
        P(None, "seq"),
    )
    out_specs = P(("clip", "seq"), None, None)
    return jax.shard_map(body, mesh=mesh, in_specs=in_specs, out_specs=out_specs, check_vma=False)
```

```python
import functools
import itertools

import jax
import jax.numpy as jnp
from jax import lax
from jax.experimental import pallas as pl
from jax.experimental.pallas import tpu as pltpu
from jax.sharding import PartitionSpec as P

D = 1280
HEADS = 10
HEAD = 64
INNER = 640
PIX = 128
NX, NZ, NY = 4, 8, 4
SEQ = NX * NZ * NY
EPS = 1e-05
BF = jnp.bfloat16
F32 = jnp.float32
SHIFTS = (0, 1, 3, 2)
GROUP = 7
TILES = 2 * GROUP


def seq_of(x, z, y):
    return (x * NZ + z) * NY + y


Z_GROUPS = [[seq_of(x, z, y) for z in range(NZ)] for x in range(NX) for y in range(NY)]
SWAP = [(i, (i + SEQ) % (2 * SEQ)) for i in range(2 * SEQ)]


def ring_perm(k, stage):
    pairs = []
    for c, x, z, y in itertools.product(range(2), range(NX), range(NZ), range(NY)):
        if (c + stage) % 2 == 0:
            to = ((x + k) % NX, z, y)
        else:
            to = (x, z, (y + k) % NY)
        pairs.append((c * SEQ + seq_of(x, z, y), c * SEQ + seq_of(*to)))
    return pairs


def ring(block, stage):
    return [block] + [
        lax.ppermute(block, ("clip", "seq"), ring_perm(k, stage)) for k in SHIFTS[1:]
    ]


def ring_by_halves(pair, stage):
    def shift(part, k):
        return lax.ppermute(part, ("clip", "seq"), ring_perm(k, stage))

    one, two = pair
    up_one, down_two = shift(one, 1), shift(two, 3)
    up_two, down_one = shift(two, 1), shift(one, 3)
    far_one, far_two = shift(up_one, 1), shift(down_two, 3)
    return [one, two, up_one, up_two, down_one, down_two, far_one, far_two]


def swap(block):
    return lax.ppermute(block, ("clip", "seq"), SWAP)


def vmem(n):
    return [pl.BlockSpec(memory_space=pltpu.VMEM)] * n


ANY = pl.BlockSpec(memory_space=pl.ANY)


def small(mib):
    return pltpu.CompilerParams(vmem_limit_bytes=mib * 1024 * 1024)


def layer_norm(x, gain):
    mean = jnp.mean(x, axis=-1, keepdims=True)
    d = x - mean
    var = jnp.mean(d * d, axis=-1, keepdims=True)
    return (d * lax.rsqrt(var + EPS) * gain).astype(BF)


def pack_kernel(ws_in, ref_in, wo_in, wt_in, wu_in, out, ws, ref, wo, wt, wu, sems):
    c = lax.axis_index("clip")
    pairs = ((ws_in, ws), (ref_in, ref), (wo_in, wo), (wt_in, wt), (wu_in, wu))
    copies = [pltpu.make_async_copy(src, dst, sems.at[i]) for i, (src, dst) in enumerate(pairs)]
    for copy in copies:
        copy.start()
    for copy in copies:
        copy.wait()

    def tile(*rows):
        n = sum(r.shape[0] for r in rows)
        parts = [r.astype(F32) for r in rows]
        if n < 16:
            parts.append(jnp.zeros((16 - n, 128), F32))
        return jnp.concatenate(parts, axis=0).astype(BF)

    def lane(ref, t):
        return ref[:, 128 * t : 128 * (t + 1)]

    def fill(half):
        refs = [lane(ref, u) for u in range(10)]
        def put(at, value):
            for z in range(NZ):
                out[z, at] = value

        for t in range(5):
            put(t, tile(lane(ws, 5 * half + t), refs[t]))
            put(GROUP + t, tile(lane(wt, 5 * half + t)))
        for at, w, extra in ((5, wo, refs[5:]), (GROUP + 5, wu, [])):
            middle = lane(w, 2).astype(F32)[5 * half : 5 * half + 5]
            put(at, tile(lane(w, 3 * half), middle))
            put(at + 1, tile(lane(w, 3 * half + 1), *extra))

    for half in range(2):
        pl.when(c == half)(functools.partial(fill, half))


def halves_kernel(along_z, p1, p2, p3, one, two):
    spatial = (along_z, p1, p2, p3)
    for half, out in enumerate((one, two)):
        for i in range(2):
            out[8 * i : 8 * i + 8] = spatial[2 * half + i][:, 0:GROUP]
        out[16:20] = along_z[4 * half : 4 * half + 4, GROUP : 2 * GROUP]


def temporal_blocks_kernel(*refs):
    out = refs[-1]
    for i, piece in enumerate(refs[:-1]):
        out[4 * i : 4 * i + 4] = piece[16:20]


def gate_kernel(*refs):
    pass


def gate(values, after):
    n = len(values)
    return list(
        pl.pallas_call(
            gate_kernel,
            out_shape=[jax.ShapeDtypeStruct(v.shape, v.dtype) for v in values],
            in_specs=vmem(n + 1),
            out_specs=vmem(n),
            input_output_aliases={i: i for i in range(n)},
            compiler_params=small(4),
            name="gate",
        )(*values, after)
    )


def reorder(kernel, args, outs, name):
    return pl.pallas_call(
        kernel,
        out_shape=[jax.ShapeDtypeStruct(n + (16, 128), BF) for n in outs],
        in_specs=vmem(len(args)),
        out_specs=vmem(len(outs)),
        compiler_params=small(8),
        name=name,
    )(*args)


def to_rows(value, out, rows, n):
    wide = 2 * out.shape[1]
    for t in range(wide):
        at = pl.ds(t, 128, stride=wide)
        rows[at, :] = value[:, 128 * t : 128 * (t + 1)] if t < n else jnp.zeros((128, 128), F32)
    out.reshape(128 * wide, 128)[...] = rows[...].astype(BF)


def from_rows(ref, rows, n):
    wide = 2 * ref.shape[1]
    rows[...] = ref.reshape(128 * wide, 128)[...].astype(F32)
    return jnp.concatenate(
        [rows[pl.ds(t, 128, stride=wide), :] for t in range(n)], axis=1
    ).astype(BF)


def place():
    s = lax.axis_index("seq")
    return lax.axis_index("clip"), s // (NZ * NY), lax.rem(s, NY)


def blocks(refs, j, i):
    each = 16 // len(refs)
    at = 4 * j + i
    return refs[at // each], 8 * (at % each)


def lanes(refs, j, i, first, count):
    ref, start = blocks(refs, j, i)
    parts = [ref[start : start + 8, first + t].reshape(128, 128) for t in range(count)]
    return jnp.concatenate(parts, axis=1)


def pieces_of(own, oth, j, first, count):
    wa = [lanes(own, j, i, first, count) for i in range(4)]
    wb = [lanes(oth, i, j, first, count) for i in range(4)]
    return jnp.concatenate(wa, axis=0), jnp.concatenate(wb, axis=0)


def spread(acc, r, j, row, x_core):
    c, x, y = place()
    for i in range(4):
        dx = jnp.where(c == x_core, SHIFTS[i], SHIFTS[j])
        dy = jnp.where(c == x_core, SHIFTS[j], SHIFTS[i])
        xs = lax.rem(x - dx + NX, NX)
        ys = lax.rem(y - dy + NY, NY)
        for z in range(NZ):
            at = (i * 8 + z) * 16
            acc[xs, z, ys, row : row + 16, :] = r[at : at + 16]


NT = (((1,), (1,)), ((), ()))
NN = (((1,), (0,)), ((), ()))


def dot(a, b, dims):
    return lax.dot_general(a, b, dims, preferred_element_type=F32)


def compact(acc, rows):
    for s in range(SEQ):
        x, z, y = s // 32, (s // 4) % 8, s % 4
        rows[15 * s : 15 * s + 15, :] = acc[x, z, y, 0:15, :]


def qkv_project(own, oth, acc, rows, tokens, x_core):
    c, _, _ = place()
    both = jnp.concatenate(halves(tokens, c), axis=1)
    for j in range(4):
        w = jnp.concatenate(pieces_of(own, oth, j, 0, 5), axis=1)
        spread(acc, dot(w, both, NT), j, 0, x_core)
    compact(acc, rows)


def out_project(own, oth, acc, rows, attn, x_core):
    c, _, _ = place()
    lo, mid, hi = attn[0:256, :], attn[256:384, :], attn[384:640, :]
    mid = jnp.concatenate([mid, jnp.zeros_like(mid)], axis=0)
    xa = jnp.concatenate([jnp.where(c == 0, lo, hi), mid], axis=1)
    xb = jnp.concatenate([jnp.where(c == 0, hi, lo), mid], axis=1)
    upper = lax.rem(lax.broadcasted_iota(jnp.int32, (512, 128), 0), 16) < 10
    for j in range(4):
        wa, wb = pieces_of(own, oth, j, 0, 2)
        ra, rb = dot(wa, xa, NN), dot(wb, xb, NN)
        ma, mb = ra[:, 128:], rb[:, 128:]
        m0, m1 = jnp.where(c == 0, ma, mb), jnp.where(c == 0, mb, ma)
        spread(acc, jnp.where(upper, ra[:, :128] + rb[:, :128], m0), j, 0, x_core)
        spread(acc, m1, j, 16, x_core)
    for s in range(SEQ):
        x, z, y = s // 32, (s // 4) % 8, s % 4
        m0 = acc[x, z, y, 10:15, :]
        m1 = acc[x, z, y, 26:31, :]
        rows[10 * s : 10 * s + 10, :] = acc[x, z, y, 0:10, :] + jnp.concatenate([m0, m1], axis=0)


def halves(xv, c):
    lo, hi = xv[:, :640], xv[:, 640:]
    first = c == 0
    return jnp.where(first, lo, hi), jnp.where(first, hi, lo)


def heads(rows, scores, attn):
    keys = scores.shape[1]
    for h in range(HEADS):
        q = rows[64 * h : 64 * (h + 1), 0:128].astype(BF)
        k = rows[640 + 64 * h : 640 + 64 * (h + 1), 0:keys].astype(BF)
        scores[h] = dot(k, q, (((0,), (0,)), ((), ())))
    for h in range(HEADS):
        st = scores[h] * (HEAD**-0.5)
        e = jnp.exp(st - jnp.max(st, axis=0, keepdims=True))
        p = (e * (1.0 / jnp.sum(e, axis=0, keepdims=True))).astype(BF)
        v = rows[1280 + 64 * h : 1280 + 64 * (h + 1), 0:keys].astype(BF)
        attn[64 * h : 64 * (h + 1), :] = dot(v, p, NN)


def reference_tokens(own, last):
    parts = []
    for t in (0, 1, 2, 3, 4, 6):
        for j in range(4):
            for i in range(4):
                at = (j * 4 + i) * 64
                ref, start = blocks(own, j, i)
                tail = ref[start : start + 8, t].astype(F32)[:, 8:16, :]
                last[t, at : at + 64, :] = tail.reshape(64, 128)
        at = (7,) if t < 5 else (2, 3, 4, 5, 6)
        parts += [last[t, pl.ds(r, 128, stride=8), :] for r in at]
    return jnp.concatenate(parts, axis=1).astype(BF)


def spatial_kernel(*refs):
    own, oth = refs[0:8], refs[8:16]
    latents, gain_s, gain_t, hidden, tnormed, acc, rows, last, attn, scores, acc_out, rows_out = refs[16:]
    normed = layer_norm(latents[...].astype(F32), gain_s[...])
    tokens = jnp.concatenate([normed, reference_tokens(own, last)], axis=0)
    qkv_project(own, oth, acc, rows, tokens, 0)
    heads(rows, scores, attn)
    views = [[p.at[:, pl.ds(5, 2)] for p in pieces] for pieces in (own, oth)]
    out_project(*views, acc_out, rows_out, attn[...].astype(BF), 0)
    h = (latents[...].astype(F32) + rows_out[...].T).astype(BF)
    hidden[...] = h
    to_rows(layer_norm(h.astype(F32), gain_t[...]).astype(F32), tnormed, rows_out, 10)


def half_kernel(*refs):
    own, (tokens, out, rest, wide) = refs[0:4], refs[4:]
    c, _, _ = place()
    xa, xb = halves(from_rows(tokens, wide, 10), c)
    rest[...] = xb
    for j in range(4):
        wa = jnp.concatenate([lanes(own, j, i, 0, 5) for i in range(4)], axis=0)
        out[512 * j : 512 * (j + 1), :] = dot(wa, xa, NT)


def temporal_kernel(*refs):
    oth = refs[0:4]
    half, rest, out, acc, rows, attn, scores, wide_out = refs[4:]
    for j in range(4):
        wb = jnp.concatenate([lanes(oth, i, j, 0, 5) for i in range(4)], axis=0)
        spread(acc, half[512 * j : 512 * (j + 1), :] + dot(wb, rest[...], NT), j, 0, 1)
    compact(acc, rows)
    heads(rows, scores, attn)
    to_rows(attn[...].T, out, wide_out, 5)


def mixed_kernel(*refs):
    own, oth = refs[0:4], refs[4:8]
    attn, hidden, mixed, acc, rows, wide, own_tiles, oth_tiles, sems = refs[8:]
    copies = [
        pltpu.make_async_copy(src.at[:, pl.ds(5, 2)], dst, sems.at[i])
        for i, (src, dst) in enumerate(((own[0], own_tiles), (oth[0], oth_tiles)))
    ]
    for copy in copies:
        copy.start()
    a = from_rows(attn, wide, 5).astype(F32).T.astype(BF)
    for copy in copies:
        copy.wait()
    views = [
        [first] + [p.at[:, pl.ds(5, 2)] for p in rest]
        for first, rest in ((own_tiles, own[1:]), (oth_tiles, oth[1:]))
    ]
    out_project(*views, acc, rows, a, 1)
    mixed[...] = (hidden[...].astype(F32) + rows[...].T).astype(BF)


def call(kernel, args, outs, scratch, name, flops, mib, dtypes=(BF, BF)):
    shapes = [jax.ShapeDtypeStruct(s, d) for s, d in zip(outs, dtypes)]
    single = len(shapes) == 1
    size = sum(a.size * a.dtype.itemsize for a in args) + sum(2 * s.size for s in shapes)
    return pl.pallas_call(
        kernel,
        out_shape=shapes[0] if single else shapes,
        in_specs=vmem(len(args)),
        out_specs=vmem(1)[0] if single else vmem(len(shapes)),
        scratch_shapes=[pltpu.VMEM(s, F32) for s in scratch],
        compiler_params=small(mib),
        cost_estimate=pl.CostEstimate(flops=flops, bytes_accessed=size, transcendentals=0),
        name=name,
    )(*args)


def body(latents, ref_hidden, gain_s, w_s, w_o, gain_t, w_t, w_u):
    latents = latents.reshape(PIX, D)
    gain_s = gain_s.reshape(1, D)
    gain_t = gain_t.reshape(1, D)
    shards = [w_s.T, ref_hidden, w_o.T, w_t.T, w_u.T]
    packed = pl.pallas_call(
        pack_kernel,
        out_shape=jax.ShapeDtypeStruct((NZ, TILES, 16, 128), BF),
        in_specs=[ANY] * 5,
        out_specs=vmem(1)[0],
        scratch_shapes=[pltpu.VMEM(a.shape, BF) for a in shards] + [pltpu.SemaphoreType.DMA((5,))],
        compiler_params=small(60),
        name="pack",
    )(*shards)
    along_z = lax.all_to_all(
        packed,
        "seq",
        0,
        0,
        axis_index_groups=Z_GROUPS,
        tiled=True,
    )
    first = ring(along_z[:, :GROUP], 0)
    own_s = ring_by_halves(reorder(halves_kernel, [along_z] + first[1:], [(20, GROUP)] * 2, "halves"), 1)
    oth_s = [swap(b) for b in own_s]
    (part_t,) = reorder(temporal_blocks_kernel, own_s, [(32, GROUP)], "temporal_blocks")
    ring_t = ring(part_t, 0)

    hidden, tnormed = call(
        spatial_kernel,
        own_s + oth_s + [latents, gain_s, gain_t],
        [(PIX, D), (PIX, 5, 2, 128)],
        [
            (NX, NZ, NY, 16, 256),
            (1920, 256),
            (GROUP, 1024, 128),
            (INNER, 128),
            (HEADS, 256, 128),
            (NX, NZ, NY, 32, 128),
            (D, 128),
        ],
        "spatial",
        9 * 10**9,
        32,
    )
    tokens = lax.all_to_all(tnormed, "seq", 0, 0, tiled=True)
    own_t = ring_t[:1] + gate(ring_t[1:], tokens)
    oth_t = [swap(ring_t[0])] + [swap(b) for b in own_t[1:]]
    half_t, rest = call(
        half_kernel,
        own_t + [tokens],
        [(2048, 128), (PIX, INNER)],
        [(D, 128)],
        "half",
        3 * 10**9,
        16,
        [F32, BF],
    )
    tattn = call(
        temporal_kernel,
        oth_t + [half_t, rest],
        [(PIX, 3, 2, 128)],
        [
            (NX, NZ, NY, 16, 128),
            (1920, 128),
            (INNER, 128),
            (HEADS, 128, 128),
            (768, 128),
        ],
        "temporal",
        5 * 10**9,
        16,
    )
    back = lax.all_to_all(tattn, "seq", 0, 0, tiled=True)
    mixed = pl.pallas_call(
        mixed_kernel,
        out_shape=jax.ShapeDtypeStruct((PIX, D), BF),
        in_specs=([ANY] + vmem(3)) * 2 + vmem(2),
        out_specs=vmem(1)[0],
        scratch_shapes=[
            pltpu.VMEM((NX, NZ, NY, 32, 128), F32),
            pltpu.VMEM((D, 128), F32),
            pltpu.VMEM((768, 128), F32),
            pltpu.VMEM((32, 2, 16, 128), BF),
            pltpu.VMEM((32, 2, 16, 128), BF),
            pltpu.SemaphoreType.DMA((2,)),
        ],
        compiler_params=small(16),
        cost_estimate=pl.CostEstimate(flops=3 * 10**9, bytes_accessed=10**7, transcendentals=0),
        name="mixed",
    )(*own_t, *oth_t, back, hidden)
    return mixed.reshape(1, PIX, D)


def solution(mesh):
    in_specs = (
        P(("clip", "seq"), None, None),
        P(("clip", "seq"), None),
        P(),
        P(None, "seq"),
        P(None, "seq"),
        P(),
        P(None, "seq"),
        P(None, "seq"),
    )
    out_specs = P(("clip", "seq"), None, None)
    return jax.shard_map(body, mesh=mesh, in_specs=in_specs, out_specs=out_specs, check_vma=False)
```

```python
import functools
import itertools

import jax
import jax.numpy as jnp
from jax import lax
from jax.experimental import pallas as pl
from jax.experimental.pallas import tpu as pltpu
from jax.sharding import PartitionSpec as P

D = 1280
HEADS = 10
HEAD = 64
INNER = 640
PIX = 128
NX, NZ, NY = 4, 8, 4
SEQ = NX * NZ * NY
EPS = 1e-05
BF = jnp.bfloat16
F32 = jnp.float32
SHIFTS = (0, 1, 3, 2)
GROUP = 7
TILES = 2 * GROUP


def seq_of(x, z, y):
    return (x * NZ + z) * NY + y


Z_GROUPS = [[seq_of(x, z, y) for z in range(NZ)] for x in range(NX) for y in range(NY)]
SWAP = [(i, (i + SEQ) % (2 * SEQ)) for i in range(2 * SEQ)]


def ring_perm(k, stage):
    pairs = []
    for c, x, z, y in itertools.product(range(2), range(NX), range(NZ), range(NY)):
        if (c + stage) % 2 == 0:
            to = ((x + k) % NX, z, y)
        else:
            to = (x, z, (y + k) % NY)
        pairs.append((c * SEQ + seq_of(x, z, y), c * SEQ + seq_of(*to)))
    return pairs


def ring(block, stage):
    return [block] + [
        lax.ppermute(block, ("clip", "seq"), ring_perm(k, stage)) for k in SHIFTS[1:]
    ]


def ring_by_halves(pair, stage):
    def shift(part, k):
        return lax.ppermute(part, ("clip", "seq"), ring_perm(k, stage))

    one, two = pair
    up_one, down_two = shift(one, 1), shift(two, 3)
    up_two, down_one = shift(two, 1), shift(one, 3)
    far_one, far_two = shift(up_one, 1), shift(down_two, 3)
    return [one, two, up_one, up_two, down_one, down_two, far_one, far_two]


def swap(block):
    return lax.ppermute(block, ("clip", "seq"), SWAP)


def vmem(n):
    return [pl.BlockSpec(memory_space=pltpu.VMEM)] * n


ANY = pl.BlockSpec(memory_space=pl.ANY)


def small(mib):
    return pltpu.CompilerParams(vmem_limit_bytes=mib * 1024 * 1024)


def layer_norm(x, gain):
    mean = jnp.mean(x, axis=-1, keepdims=True)
    d = x - mean
    var = jnp.mean(d * d, axis=-1, keepdims=True)
    return (d * lax.rsqrt(var + EPS) * gain).astype(BF)


def pack_kernel(ws_in, ref_in, wo_in, wt_in, wu_in, out, ws, ref, wo, wt, wu, sems):
    c = lax.axis_index("clip")
    pairs = ((ws_in, ws), (ref_in, ref), (wo_in, wo), (wt_in, wt), (wu_in, wu))
    copies = [pltpu.make_async_copy(src, dst, sems.at[i]) for i, (src, dst) in enumerate(pairs)]
    for copy in copies:
        copy.start()
    for copy in copies:
        copy.wait()

    def tile(*rows):
        n = sum(r.shape[0] for r in rows)
        parts = [r.astype(F32) for r in rows]
        if n < 16:
            parts.append(jnp.zeros((16 - n, 128), F32))
        return jnp.concatenate(parts, axis=0).astype(BF)

    def lane(ref, t):
        return ref[:, 128 * t : 128 * (t + 1)]

    def fill(half):
        refs = [lane(ref, u) for u in range(10)]
        def put(at, value):
            for z in range(NZ):
                out[z, at] = value

        for t in range(5):
            put(t, tile(lane(ws, 5 * half + t), refs[t]))
            put(GROUP + t, tile(lane(wt, 5 * half + t)))
        for at, w, extra in ((5, wo, refs[5:]), (GROUP + 5, wu, [])):
            middle = lane(w, 2).astype(F32)[5 * half : 5 * half + 5]
            put(at, tile(lane(w, 3 * half), middle))
            put(at + 1, tile(lane(w, 3 * half + 1), *extra))

    for half in range(2):
        pl.when(c == half)(functools.partial(fill, half))


def halves_kernel(along_z, p1, p2, p3, after, one, two):
    spatial = (along_z, p1, p2, p3)
    for half, out in enumerate((one, two)):
        for i in range(2):
            out[8 * i : 8 * i + 8] = spatial[2 * half + i][:, 0:GROUP]
        out[16:20] = along_z[4 * half : 4 * half + 4, GROUP : 2 * GROUP]


def temporal_blocks_kernel(*refs):
    out = refs[-1]
    for i, piece in enumerate(refs[:-1]):
        out[4 * i : 4 * i + 4] = piece[16:20]


def gate_kernel(*refs):
    pass


def gate(values, after):
    n = len(values)
    return list(
        pl.pallas_call(
            gate_kernel,
            out_shape=[jax.ShapeDtypeStruct(v.shape, v.dtype) for v in values],
            in_specs=vmem(n + 1),
            out_specs=vmem(n),
            input_output_aliases={i: i for i in range(n)},
            compiler_params=small(4),
            name="gate",
        )(*values, after)
    )


def reorder(kernel, args, outs, name):
    return pl.pallas_call(
        kernel,
        out_shape=[jax.ShapeDtypeStruct(n + (16, 128), BF) for n in outs],
        in_specs=vmem(len(args)),
        out_specs=vmem(len(outs)),
        compiler_params=small(8),
        name=name,
    )(*args)


def to_rows(value, out, rows, n):
    wide = 2 * out.shape[1]
    for t in range(wide):
        at = pl.ds(t, 128, stride=wide)
        rows[at, :] = value[:, 128 * t : 128 * (t + 1)] if t < n else jnp.zeros((128, 128), F32)
    out.reshape(128 * wide, 128)[...] = rows[...].astype(BF)


def from_rows(ref, rows, n):
    wide = 2 * ref.shape[1]
    rows[...] = ref.reshape(128 * wide, 128)[...].astype(F32)
    return jnp.concatenate(
        [rows[pl.ds(t, 128, stride=wide), :] for t in range(n)], axis=1
    ).astype(BF)


def place():
    s = lax.axis_index("seq")
    return lax.axis_index("clip"), s // (NZ * NY), lax.rem(s, NY)


def blocks(refs, j, i):
    each = 16 // len(refs)
    at = 4 * j + i
    return refs[at // each], 8 * (at % each)


def lanes(refs, j, i, first, count):
    ref, start = blocks(refs, j, i)
    parts = [ref[start : start + 8, first + t].reshape(128, 128) for t in range(count)]
    return jnp.concatenate(parts, axis=1)


def pieces_of(own, oth, j, first, count):
    wa = [lanes(own, j, i, first, count) for i in range(4)]
    wb = [lanes(oth, i, j, first, count) for i in range(4)]
    return jnp.concatenate(wa, axis=0), jnp.concatenate(wb, axis=0)


def spread(acc, r, j, row, x_core):
    c, x, y = place()
    for i in range(4):
        dx = jnp.where(c == x_core, SHIFTS[i], SHIFTS[j])
        dy = jnp.where(c == x_core, SHIFTS[j], SHIFTS[i])
        xs = lax.rem(x - dx + NX, NX)
        ys = lax.rem(y - dy + NY, NY)
        for z in range(NZ):
            at = (i * 8 + z) * 16
            acc[xs, z, ys, row : row + 16, :] = r[at : at + 16]


NT = (((1,), (1,)), ((), ()))
NN = (((1,), (0,)), ((), ()))


def dot(a, b, dims):
    return lax.dot_general(a, b, dims, preferred_element_type=F32)


def compact(acc, rows):
    for s in range(SEQ):
        x, z, y = s // 32, (s // 4) % 8, s % 4
        rows[15 * s : 15 * s + 15, :] = acc[x, z, y, 0:15, :]


def qkv_project(own, oth, acc, rows, tokens, x_core):
    c, _, _ = place()
    both = jnp.concatenate(halves(tokens, c), axis=1)
    for j in range(4):
        w = jnp.concatenate(pieces_of(own, oth, j, 0, 5), axis=1)
        spread(acc, dot(w, both, NT), j, 0, x_core)
    compact(acc, rows)


def out_project(own, oth, acc, rows, attn, x_core):
    c, _, _ = place()
    lo, mid, hi = attn[0:256, :], attn[256:384, :], attn[384:640, :]
    mid = jnp.concatenate([mid, jnp.zeros_like(mid)], axis=0)
    xa = jnp.concatenate([jnp.where(c == 0, lo, hi), mid], axis=1)
    xb = jnp.concatenate([jnp.where(c == 0, hi, lo), mid], axis=1)
    upper = lax.rem(lax.broadcasted_iota(jnp.int32, (512, 128), 0), 16) < 10
    for j in range(4):
        wa, wb = pieces_of(own, oth, j, 0, 2)
        ra, rb = dot(wa, xa, NN), dot(wb, xb, NN)
        ma, mb = ra[:, 128:], rb[:, 128:]
        m0, m1 = jnp.where(c == 0, ma, mb), jnp.where(c == 0, mb, ma)
        spread(acc, jnp.where(upper, ra[:, :128] + rb[:, :128], m0), j, 0, x_core)
        spread(acc, m1, j, 16, x_core)
    for s in range(SEQ):
        x, z, y = s // 32, (s // 4) % 8, s % 4
        m0 = acc[x, z, y, 10:15, :]
        m1 = acc[x, z, y, 26:31, :]
        rows[10 * s : 10 * s + 10, :] = acc[x, z, y, 0:10, :] + jnp.concatenate([m0, m1], axis=0)


def halves(xv, c):
    lo, hi = xv[:, :640], xv[:, 640:]
    first = c == 0
    return jnp.where(first, lo, hi), jnp.where(first, hi, lo)


def heads(rows, scores, attn):
    keys = scores.shape[1]
    for h in range(HEADS):
        q = rows[64 * h : 64 * (h + 1), 0:128].astype(BF)
        k = rows[640 + 64 * h : 640 + 64 * (h + 1), 0:keys].astype(BF)
        scores[h] = dot(k, q, (((0,), (0,)), ((), ())))
    for h in range(HEADS):
        st = scores[h] * (HEAD**-0.5)
        e = jnp.exp(st - jnp.max(st, axis=0, keepdims=True))
        p = (e * (1.0 / jnp.sum(e, axis=0, keepdims=True))).astype(BF)
        v = rows[1280 + 64 * h : 1280 + 64 * (h + 1), 0:keys].astype(BF)
        attn[64 * h : 64 * (h + 1), :] = dot(v, p, NN)


def reference_tokens(own, last):
    parts = []
    for t in (0, 1, 2, 3, 4, 6):
        for j in range(4):
            for i in range(4):
                at = (j * 4 + i) * 64
                ref, start = blocks(own, j, i)
                tail = ref[start : start + 8, t].astype(F32)[:, 8:16, :]
                last[t, at : at + 64, :] = tail.reshape(64, 128)
        at = (7,) if t < 5 else (2, 3, 4, 5, 6)
        parts += [last[t, pl.ds(r, 128, stride=8), :] for r in at]
    return jnp.concatenate(parts, axis=1).astype(BF)


def norm_kernel(latents, gain, out):
    out[...] = layer_norm(latents[...].astype(F32), gain[...])


def spatial_kernel(*refs):
    own, oth = refs[0:8], refs[8:16]
    latents, normed, gain_t, hidden, tnormed, acc, rows, last, attn, scores, acc_out, rows_out = refs[16:]
    tokens = jnp.concatenate([normed[...], reference_tokens(own, last)], axis=0)
    qkv_project(own, oth, acc, rows, tokens, 0)
    heads(rows, scores, attn)
    views = [[p.at[:, pl.ds(5, 2)] for p in pieces] for pieces in (own, oth)]
    out_project(*views, acc_out, rows_out, attn[...].astype(BF), 0)
    h = (latents[...].astype(F32) + rows_out[...].T).astype(BF)
    hidden[...] = h
    to_rows(layer_norm(h.astype(F32), gain_t[...]).astype(F32), tnormed, rows_out, 10)


def half_kernel(*refs):
    own, (tokens, out, rest, wide) = refs[0:4], refs[4:]
    c, _, _ = place()
    xa, xb = halves(from_rows(tokens, wide, 10), c)
    rest[...] = xb
    for j in range(4):
        wa = jnp.concatenate([lanes(own, j, i, 0, 5) for i in range(4)], axis=0)
        out[512 * j : 512 * (j + 1), :] = dot(wa, xa, NT)


def temporal_kernel(*refs):
    oth = refs[0:4]
    half, rest, out, acc, rows, attn, scores, wide_out = refs[4:]
    for j in range(4):
        wb = jnp.concatenate([lanes(oth, i, j, 0, 5) for i in range(4)], axis=0)
        spread(acc, half[512 * j : 512 * (j + 1), :] + dot(wb, rest[...], NT), j, 0, 1)
    compact(acc, rows)
    heads(rows, scores, attn)
    to_rows(attn[...].T, out, wide_out, 5)


def mixed_kernel(*refs):
    own, oth = refs[0:4], refs[4:8]
    attn, hidden, mixed, acc, rows, wide, own_tiles, oth_tiles, sems = refs[8:]
    copies = [
        pltpu.make_async_copy(src.at[:, pl.ds(5, 2)], dst, sems.at[i])
        for i, (src, dst) in enumerate(((own[0], own_tiles), (oth[0], oth_tiles)))
    ]
    for copy in copies:
        copy.start()
    a = from_rows(attn, wide, 5).astype(F32).T.astype(BF)
    for copy in copies:
        copy.wait()
    views = [
        [first] + [p.at[:, pl.ds(5, 2)] for p in rest]
        for first, rest in ((own_tiles, own[1:]), (oth_tiles, oth[1:]))
    ]
    out_project(*views, acc, rows, a, 1)
    mixed[...] = (hidden[...].astype(F32) + rows[...].T).astype(BF)


def call(kernel, args, outs, scratch, name, flops, mib, dtypes=(BF, BF)):
    shapes = [jax.ShapeDtypeStruct(s, d) for s, d in zip(outs, dtypes)]
    single = len(shapes) == 1
    size = sum(a.size * a.dtype.itemsize for a in args) + sum(2 * s.size for s in shapes)
    return pl.pallas_call(
        kernel,
        out_shape=shapes[0] if single else shapes,
        in_specs=vmem(len(args)),
        out_specs=vmem(1)[0] if single else vmem(len(shapes)),
        scratch_shapes=[pltpu.VMEM(s, F32) for s in scratch],
        compiler_params=small(mib),
        cost_estimate=pl.CostEstimate(flops=flops, bytes_accessed=size, transcendentals=0),
        name=name,
    )(*args)


def body(latents, ref_hidden, gain_s, w_s, w_o, gain_t, w_t, w_u):
    latents = latents.reshape(PIX, D)
    gain_s = gain_s.reshape(1, D)
    gain_t = gain_t.reshape(1, D)
    shards = [w_s.T, ref_hidden, w_o.T, w_t.T, w_u.T]
    packed = pl.pallas_call(
        pack_kernel,
        out_shape=jax.ShapeDtypeStruct((NZ, TILES, 16, 128), BF),
        in_specs=[ANY] * 5,
        out_specs=vmem(1)[0],
        scratch_shapes=[pltpu.VMEM(a.shape, BF) for a in shards] + [pltpu.SemaphoreType.DMA((5,))],
        compiler_params=small(60),
        name="pack",
    )(*shards)
    along_z = lax.all_to_all(
        packed,
        "seq",
        0,
        0,
        axis_index_groups=Z_GROUPS,
        tiled=True,
    )
    first = ring(along_z[:, :GROUP], 0)
    normed = call(norm_kernel, [latents, gain_s], [(PIX, D)], [], "norm", 10**9, 4)
    args = [along_z] + first[1:] + [normed]
    own_s = ring_by_halves(reorder(halves_kernel, args, [(20, GROUP)] * 2, "halves"), 1)
    oth_s = [swap(b) for b in own_s]
    (part_t,) = reorder(temporal_blocks_kernel, own_s, [(32, GROUP)], "temporal_blocks")
    ring_t = ring(part_t, 0)

    hidden, tnormed = call(
        spatial_kernel,
        own_s + oth_s + [latents, normed, gain_t],
        [(PIX, D), (PIX, 5, 2, 128)],
        [
            (NX, NZ, NY, 16, 256),
            (1920, 256),
            (GROUP, 1024, 128),
            (INNER, 128),
            (HEADS, 256, 128),
            (NX, NZ, NY, 32, 128),
            (D, 128),
        ],
        "spatial",
        9 * 10**9,
        32,
    )
    tokens = lax.all_to_all(tnormed, "seq", 0, 0, tiled=True)
    own_t = ring_t[:1] + gate(ring_t[1:], tokens)
    oth_t = [swap(ring_t[0])] + [swap(b) for b in own_t[1:]]
    half_t, rest = call(
        half_kernel,
        own_t + [tokens],
        [(2048, 128), (PIX, INNER)],
        [(D, 128)],
        "half",
        3 * 10**9,
        16,
        [F32, BF],
    )
    tattn = call(
        temporal_kernel,
        oth_t + [half_t, rest],
        [(PIX, 3, 2, 128)],
        [
            (NX, NZ, NY, 16, 128),
            (1920, 128),
            (INNER, 128),
            (HEADS, 128, 128),
            (768, 128),
        ],
        "temporal",
        5 * 10**9,
        16,
    )
    back = lax.all_to_all(tattn, "seq", 0, 0, tiled=True)
    mixed = pl.pallas_call(
        mixed_kernel,
        out_shape=jax.ShapeDtypeStruct((PIX, D), BF),
        in_specs=([ANY] + vmem(3)) * 2 + vmem(2),
        out_specs=vmem(1)[0],
        scratch_shapes=[
            pltpu.VMEM((NX, NZ, NY, 32, 128), F32),
            pltpu.VMEM((D, 128), F32),
            pltpu.VMEM((768, 128), F32),
            pltpu.VMEM((32, 2, 16, 128), BF),
            pltpu.VMEM((32, 2, 16, 128), BF),
            pltpu.SemaphoreType.DMA((2,)),
        ],
        compiler_params=small(16),
        cost_estimate=pl.CostEstimate(flops=3 * 10**9, bytes_accessed=10**7, transcendentals=0),
        name="mixed",
    )(*own_t, *oth_t, back, hidden)
    return mixed.reshape(1, PIX, D)


def solution(mesh):
    in_specs = (
        P(("clip", "seq"), None, None),
        P(("clip", "seq"), None),
        P(),
        P(None, "seq"),
        P(None, "seq"),
        P(),
        P(None, "seq"),
        P(None, "seq"),
    )
    out_specs = P(("clip", "seq"), None, None)
    return jax.shard_map(body, mesh=mesh, in_specs=in_specs, out_specs=out_specs, check_vma=False)
```

```python
import functools
import itertools

import jax
import jax.numpy as jnp
from jax import lax
from jax.experimental import pallas as pl
from jax.experimental.pallas import tpu as pltpu
from jax.sharding import PartitionSpec as P

D = 1280
HEADS = 10
HEAD = 64
INNER = 640
PIX = 128
NX, NZ, NY = 4, 8, 4
SEQ = NX * NZ * NY
EPS = 1e-05
BF = jnp.bfloat16
F32 = jnp.float32
SHIFTS = (0, 1, 3, 2)
GROUP = 7
TILES = 2 * GROUP


def seq_of(x, z, y):
    return (x * NZ + z) * NY + y


Z_GROUPS = [[seq_of(x, z, y) for z in range(NZ)] for x in range(NX) for y in range(NY)]
SWAP = [(i, (i + SEQ) % (2 * SEQ)) for i in range(2 * SEQ)]


def ring_perm(k, stage):
    pairs = []
    for c, x, z, y in itertools.product(range(2), range(NX), range(NZ), range(NY)):
        if (c + stage) % 2 == 0:
            to = ((x + k) % NX, z, y)
        else:
            to = (x, z, (y + k) % NY)
        pairs.append((c * SEQ + seq_of(x, z, y), c * SEQ + seq_of(*to)))
    return pairs


def ring(block, stage):
    return [block] + [
        lax.ppermute(block, ("clip", "seq"), ring_perm(k, stage)) for k in SHIFTS[1:]
    ]


def ring_by_halves(pair, stage):
    def shift(part, k):
        return lax.ppermute(part, ("clip", "seq"), ring_perm(k, stage))

    one, two = pair
    up_one, down_two = shift(one, 1), shift(two, 3)
    up_two, down_one = shift(two, 1), shift(one, 3)
    far_one, far_two = shift(up_one, 1), shift(down_two, 3)
    return [one, two, up_one, up_two, down_one, down_two, far_one, far_two]


def swap(block):
    return lax.ppermute(block, ("clip", "seq"), SWAP)


def vmem(n):
    return [pl.BlockSpec(memory_space=pltpu.VMEM)] * n


ANY = pl.BlockSpec(memory_space=pl.ANY)


def small(mib):
    return pltpu.CompilerParams(vmem_limit_bytes=mib * 1024 * 1024)


def layer_norm(x, gain):
    mean = jnp.mean(x, axis=-1, keepdims=True)
    d = x - mean
    var = jnp.mean(d * d, axis=-1, keepdims=True)
    return (d * lax.rsqrt(var + EPS) * gain).astype(BF)


def pack_kernel(ws_in, ref_in, wo_in, wt_in, wu_in, out, ws, ref, wo, wt, wu, sems):
    c = lax.axis_index("clip")
    pairs = ((ws_in, ws), (ref_in, ref), (wo_in, wo), (wt_in, wt), (wu_in, wu))
    copies = [pltpu.make_async_copy(src, dst, sems.at[i]) for i, (src, dst) in enumerate(pairs)]
    for copy in copies:
        copy.start()
    for copy in copies:
        copy.wait()

    def tile(*rows):
        n = sum(r.shape[0] for r in rows)
        parts = [r.astype(F32) for r in rows]
        if n < 16:
            parts.append(jnp.zeros((16 - n, 128), F32))
        return jnp.concatenate(parts, axis=0).astype(BF)

    def lane(ref, t):
        return ref[:, 128 * t : 128 * (t + 1)]

    def fill(half):
        refs = [lane(ref, u) for u in range(10)]
        def put(at, value):
            for z in range(NZ):
                out[z, at] = value

        for t in range(5):
            put(t, tile(lane(ws, 5 * half + t), refs[t]))
            put(GROUP + t, tile(lane(wt, 5 * half + t)))
        for at, w, extra in ((5, wo, refs[5:]), (GROUP + 5, wu, [])):
            middle = lane(w, 2).astype(F32)[5 * half : 5 * half + 5]
            put(at, tile(lane(w, 3 * half), middle))
            put(at + 1, tile(lane(w, 3 * half + 1), *extra))

    for half in range(2):
        pl.when(c == half)(functools.partial(fill, half))


def halves_kernel(along_z, p1, p2, p3, one, two):
    spatial = (along_z, p1, p2, p3)
    for half, out in enumerate((one, two)):
        for i in range(2):
            out[8 * i : 8 * i + 8] = spatial[2 * half + i][:, 0:GROUP]
        out[16:20] = along_z[4 * half : 4 * half + 4, GROUP : 2 * GROUP]


def temporal_blocks_kernel(*refs):
    out = refs[-1]
    for i, piece in enumerate(refs[:-1]):
        out[4 * i : 4 * i + 4] = piece[16:20]


def gate_kernel(*refs):
    pass


def gate(values, after):
    n = len(values)
    return list(
        pl.pallas_call(
            gate_kernel,
            out_shape=[jax.ShapeDtypeStruct(v.shape, v.dtype) for v in values],
            in_specs=vmem(n + 1),
            out_specs=vmem(n),
            input_output_aliases={i: i for i in range(n)},
            compiler_params=small(4),
            name="gate",
        )(*values, after)
    )


def reorder(kernel, args, outs, name):
    return pl.pallas_call(
        kernel,
        out_shape=[jax.ShapeDtypeStruct(n + (16, 128), BF) for n in outs],
        in_specs=vmem(len(args)),
        out_specs=vmem(len(outs)),
        compiler_params=small(8),
        name=name,
    )(*args)


def to_rows(value, out, rows, n):
    wide = 2 * out.shape[1]
    for t in range(wide):
        at = pl.ds(t, 128, stride=wide)
        rows[at, :] = value[:, 128 * t : 128 * (t + 1)] if t < n else jnp.zeros((128, 128), F32)
    out.reshape(128 * wide, 128)[...] = rows[...].astype(BF)


def from_rows(ref, rows, n):
    wide = 2 * ref.shape[1]
    rows[...] = ref.reshape(128 * wide, 128)[...].astype(F32)
    return jnp.concatenate(
        [rows[pl.ds(t, 128, stride=wide), :] for t in range(n)], axis=1
    ).astype(BF)


def place():
    s = lax.axis_index("seq")
    return lax.axis_index("clip"), s // (NZ * NY), lax.rem(s, NY)


def blocks(refs, j, i):
    each = 16 // len(refs)
    at = 4 * j + i
    return refs[at // each], 8 * (at % each)


def lanes(refs, j, i, first, count):
    ref, start = blocks(refs, j, i)
    parts = [ref[start : start + 8, first + t].reshape(128, 128) for t in range(count)]
    return jnp.concatenate(parts, axis=1)


def pieces_of(own, oth, j, first, count):
    wa = [lanes(own, j, i, first, count) for i in range(4)]
    wb = [lanes(oth, i, j, first, count) for i in range(4)]
    return jnp.concatenate(wa, axis=0), jnp.concatenate(wb, axis=0)


def spread(acc, r, j, row, x_core):
    c, x, y = place()
    for i in range(4):
        dx = jnp.where(c == x_core, SHIFTS[i], SHIFTS[j])
        dy = jnp.where(c == x_core, SHIFTS[j], SHIFTS[i])
        xs = lax.rem(x - dx + NX, NX)
        ys = lax.rem(y - dy + NY, NY)
        for z in range(NZ):
            at = (i * 8 + z) * 16
            acc[xs, z, ys, row : row + 16, :] = r[at : at + 16]


NT = (((1,), (1,)), ((), ()))
NN = (((1,), (0,)), ((), ()))


def dot(a, b, dims):
    return lax.dot_general(a, b, dims, preferred_element_type=F32)


def compact(acc, rows):
    for s in range(SEQ):
        x, z, y = s // 32, (s // 4) % 8, s % 4
        rows[15 * s : 15 * s + 15, :] = acc[x, z, y, 0:15, :]


def qkv_project(own, oth, acc, rows, tokens, x_core):
    c, _, _ = place()
    both = jnp.concatenate(halves(tokens, c), axis=1)
    for j in range(4):
        w = jnp.concatenate(pieces_of(own, oth, j, 0, 5), axis=1)
        spread(acc, dot(w, both, NT), j, 0, x_core)
    compact(acc, rows)


def out_project(own, oth, acc, rows, attn, x_core):
    c, _, _ = place()
    lo, mid, hi = attn[0:256, :], attn[256:384, :], attn[384:640, :]
    mid = jnp.concatenate([mid, jnp.zeros_like(mid)], axis=0)
    xa = jnp.concatenate([jnp.where(c == 0, lo, hi), mid], axis=1)
    xb = jnp.concatenate([jnp.where(c == 0, hi, lo), mid], axis=1)
    upper = lax.rem(lax.broadcasted_iota(jnp.int32, (512, 128), 0), 16) < 10
    for j in range(4):
        wa, wb = pieces_of(own, oth, j, 0, 2)
        ra, rb = dot(wa, xa, NN), dot(wb, xb, NN)
        ma, mb = ra[:, 128:], rb[:, 128:]
        m0, m1 = jnp.where(c == 0, ma, mb), jnp.where(c == 0, mb, ma)
        spread(acc, jnp.where(upper, ra[:, :128] + rb[:, :128], m0), j, 0, x_core)
        spread(acc, m1, j, 16, x_core)
    for s in range(SEQ):
        x, z, y = s // 32, (s // 4) % 8, s % 4
        m0 = acc[x, z, y, 10:15, :]
        m1 = acc[x, z, y, 26:31, :]
        rows[10 * s : 10 * s + 10, :] = acc[x, z, y, 0:10, :] + jnp.concatenate([m0, m1], axis=0)


def halves(xv, c):
    lo, hi = xv[:, :640], xv[:, 640:]
    first = c == 0
    return jnp.where(first, lo, hi), jnp.where(first, hi, lo)


def heads(rows, scores, attn):
    keys = scores.shape[1]
    for h in range(HEADS):
        q = (rows[64 * h : 64 * (h + 1), 0:128].astype(BF) * (HEAD**-0.5)).astype(BF)
        k = rows[640 + 64 * h : 640 + 64 * (h + 1), 0:keys].astype(BF)
        scores[h] = dot(k, q, (((0,), (0,)), ((), ())))
    for h in range(HEADS):
        st = scores[h]
        e = jnp.exp(st - jnp.max(st, axis=0, keepdims=True))
        p = (e * (1.0 / jnp.sum(e, axis=0, keepdims=True))).astype(BF)
        v = rows[1280 + 64 * h : 1280 + 64 * (h + 1), 0:keys].astype(BF)
        attn[64 * h : 64 * (h + 1), :] = dot(v, p, NN)


def reference_tokens(own, last):
    parts = []
    for t in (0, 1, 2, 3, 4, 6):
        for j in range(4):
            for i in range(4):
                at = (j * 4 + i) * 64
                ref, start = blocks(own, j, i)
                tail = ref[start : start + 8, t].astype(F32)[:, 8:16, :]
                last[t, at : at + 64, :] = tail.reshape(64, 128)
        at = (7,) if t < 5 else (2, 3, 4, 5, 6)
        parts += [last[t, pl.ds(r, 128, stride=8), :] for r in at]
    return jnp.concatenate(parts, axis=1).astype(BF)


def spatial_kernel(*refs):
    own, oth = refs[0:8], refs[8:16]
    latents, gain_s, gain_t, hidden, tnormed, acc, rows, last, attn, scores, acc_out, rows_out = refs[16:]
    normed = layer_norm(latents[...].astype(F32), gain_s[...])
    tokens = jnp.concatenate([normed, reference_tokens(own, last)], axis=0)
    qkv_project(own, oth, acc, rows, tokens, 0)
    heads(rows, scores, attn)
    views = [[p.at[:, pl.ds(5, 2)] for p in pieces] for pieces in (own, oth)]
    out_project(*views, acc_out, rows_out, attn[...].astype(BF), 0)
    h = (latents[...].astype(F32) + rows_out[...].T).astype(BF)
    hidden[...] = h
    to_rows(layer_norm(h.astype(F32), gain_t[...]).astype(F32), tnormed, rows_out, 10)


def half_kernel(*refs):
    own, (tokens, out, rest, wide) = refs[0:4], refs[4:]
    c, _, _ = place()
    xa, xb = halves(from_rows(tokens, wide, 10), c)
    rest[...] = xb
    for j in range(4):
        wa = jnp.concatenate([lanes(own, j, i, 0, 5) for i in range(4)], axis=0)
        out[512 * j : 512 * (j + 1), :] = dot(wa, xa, NT)


def temporal_kernel(*refs):
    oth = refs[0:4]
    half, rest, out, acc, rows, attn, scores, wide_out = refs[4:]
    for j in range(4):
        wb = jnp.concatenate([lanes(oth, i, j, 0, 5) for i in range(4)], axis=0)
        spread(acc, half[512 * j : 512 * (j + 1), :] + dot(wb, rest[...], NT), j, 0, 1)
    compact(acc, rows)
    heads(rows, scores, attn)
    to_rows(attn[...].T, out, wide_out, 5)


def mixed_kernel(*refs):
    own, oth = refs[0:4], refs[4:8]
    attn, hidden, mixed, acc, rows, wide, own_tiles, oth_tiles, sems = refs[8:]
    copies = [
        pltpu.make_async_copy(src.at[:, pl.ds(5, 2)], dst, sems.at[i])
        for i, (src, dst) in enumerate(((own[0], own_tiles), (oth[0], oth_tiles)))
    ]
    for copy in copies:
        copy.start()
    a = from_rows(attn, wide, 5).astype(F32).T.astype(BF)
    for copy in copies:
        copy.wait()
    views = [
        [first] + [p.at[:, pl.ds(5, 2)] for p in rest]
        for first, rest in ((own_tiles, own[1:]), (oth_tiles, oth[1:]))
    ]
    out_project(*views, acc, rows, a, 1)
    mixed[...] = (hidden[...].astype(F32) + rows[...].T).astype(BF)


def call(kernel, args, outs, scratch, name, flops, mib, dtypes=(BF, BF)):
    shapes = [jax.ShapeDtypeStruct(s, d) for s, d in zip(outs, dtypes)]
    single = len(shapes) == 1
    size = sum(a.size * a.dtype.itemsize for a in args) + sum(2 * s.size for s in shapes)
    return pl.pallas_call(
        kernel,
        out_shape=shapes[0] if single else shapes,
        in_specs=vmem(len(args)),
        out_specs=vmem(1)[0] if single else vmem(len(shapes)),
        scratch_shapes=[pltpu.VMEM(s, F32) for s in scratch],
        compiler_params=small(mib),
        cost_estimate=pl.CostEstimate(flops=flops, bytes_accessed=size, transcendentals=0),
        name=name,
    )(*args)


def body(latents, ref_hidden, gain_s, w_s, w_o, gain_t, w_t, w_u):
    latents = latents.reshape(PIX, D)
    gain_s = gain_s.reshape(1, D)
    gain_t = gain_t.reshape(1, D)
    shards = [w_s.T, ref_hidden, w_o.T, w_t.T, w_u.T]
    packed = pl.pallas_call(
        pack_kernel,
        out_shape=jax.ShapeDtypeStruct((NZ, TILES, 16, 128), BF),
        in_specs=[ANY] * 5,
        out_specs=vmem(1)[0],
        scratch_shapes=[pltpu.VMEM(a.shape, BF) for a in shards] + [pltpu.SemaphoreType.DMA((5,))],
        compiler_params=small(60),
        name="pack",
    )(*shards)
    along_z = lax.all_to_all(
        packed,
        "seq",
        0,
        0,
        axis_index_groups=Z_GROUPS,
        tiled=True,
    )
    first = ring(along_z[:, :GROUP], 0)
    own_s = ring_by_halves(reorder(halves_kernel, [along_z] + first[1:], [(20, GROUP)] * 2, "halves"), 1)
    oth_s = [swap(b) for b in own_s]
    (part_t,) = reorder(temporal_blocks_kernel, own_s, [(32, GROUP)], "temporal_blocks")
    ring_t = ring(part_t, 0)

    hidden, tnormed = call(
        spatial_kernel,
        own_s + oth_s + [latents, gain_s, gain_t],
        [(PIX, D), (PIX, 5, 2, 128)],
        [
            (NX, NZ, NY, 16, 256),
            (1920, 256),
            (GROUP, 1024, 128),
            (INNER, 128),
            (HEADS, 256, 128),
            (NX, NZ, NY, 32, 128),
            (D, 128),
        ],
        "spatial",
        9 * 10**9,
        32,
    )
    tokens = lax.all_to_all(tnormed, "seq", 0, 0, tiled=True)
    own_t = ring_t[:1] + gate(ring_t[1:], tokens)
    oth_t = [swap(ring_t[0])] + [swap(b) for b in own_t[1:]]
    half_t, rest = call(
        half_kernel,
        own_t + [tokens],
        [(2048, 128), (PIX, INNER)],
        [(D, 128)],
        "half",
        3 * 10**9,
        16,
        [F32, BF],
    )
    tattn = call(
        temporal_kernel,
        oth_t + [half_t, rest],
        [(PIX, 3, 2, 128)],
        [
            (NX, NZ, NY, 16, 128),
            (1920, 128),
            (INNER, 128),
            (HEADS, 128, 128),
            (768, 128),
        ],
        "temporal",
        5 * 10**9,
        16,
    )
    back = lax.all_to_all(tattn, "seq", 0, 0, tiled=True)
    mixed = pl.pallas_call(
        mixed_kernel,
        out_shape=jax.ShapeDtypeStruct((PIX, D), BF),
        in_specs=([ANY] + vmem(3)) * 2 + vmem(2),
        out_specs=vmem(1)[0],
        scratch_shapes=[
            pltpu.VMEM((NX, NZ, NY, 32, 128), F32),
            pltpu.VMEM((D, 128), F32),
            pltpu.VMEM((768, 128), F32),
            pltpu.VMEM((32, 2, 16, 128), BF),
            pltpu.VMEM((32, 2, 16, 128), BF),
            pltpu.SemaphoreType.DMA((2,)),
        ],
        compiler_params=small(16),
        cost_estimate=pl.CostEstimate(flops=3 * 10**9, bytes_accessed=10**7, transcendentals=0),
        name="mixed",
    )(*own_t, *oth_t, back, hidden)
    return mixed.reshape(1, PIX, D)


def solution(mesh):
    in_specs = (
        P(("clip", "seq"), None, None),
        P(("clip", "seq"), None),
        P(),
        P(None, "seq"),
        P(None, "seq"),
        P(),
        P(None, "seq"),
        P(None, "seq"),
    )
    out_specs = P(("clip", "seq"), None, None)
    return jax.shard_map(body, mesh=mesh, in_specs=in_specs, out_specs=out_specs, check_vma=False)
```
